32 devices in a mesh: dop: 8 (over z, x), rng: 4 (over y, core).
Axes of the slice: x: 2, y: 2, z: 4, core: 2. Of those that a mesh axis runs over, the one named last changes fastest.
Arguments:
- echoes: bfloat16 [2, 256, 64, 16384], P(None, 'dop', None, 'rng'), may hold values from -6 to 6
- chirp: bfloat16 [2, 512], replicated, may hold values from -0.1875 to 0.1875
- ridge: int32 [256], P('dop'), may hold values from 0 to 1, as said below
- counts: int32 [256], P('dop'), may hold values from 1 to 8
Outputs:
- whitened: bfloat16 [256, 128, 16384], P('dop', None, 'rng')
The draws below stay inside these ranges and needn't reach their ends.
Inputs may be any that keep to these rules, and one draw needn't show every extreme that they name: `ridge`: exactly 64 bins are 1 and they are consecutive, cyclically over the 256 bins.
All inputs are finite; a program needn't handle non-finite values.
Results may differ from the reference program's by a relative error of at most 0.008.
Values may be sent and summed in bfloat16 or wider, within the bound.
No kernel may reach another device: no remote copies, remote signals or barrier semaphores. Data moves between devices by JAX's collectives and lax.ppermute only.
A program may use at most 256 MiB of HBM per device.

```python
import math
import jax
import jax.numpy as jnp
from jax import lax

CHANNELS = 64
PULSES = 256
TAPS = 512
GATE_DEV = 4096
GATES = 16384
TRAIN_BLK = 512
NBLK = 8
RIDGE = 64
N_RNG = 4


def draw_ridge(key, part):
    center = jax.random.randint(key, (), 0, PULSES)
    bin_index = jnp.arange(PULSES, dtype=jnp.int32)
    return ((bin_index - center) % PULSES < RIDGE).astype(jnp.int32)


def touch_ends(values, stream_key, low, largest):
    place = [jax.random.randint(jax.random.fold_in(stream_key, axis), (), 0, length) for axis, length in enumerate(values.shape)]
    widest = values.shape.index(max(values.shape))
    neighbour = place[:widest] + [(place[widest] + 1) % values.shape[widest]] + place[widest + 1:]
    return values.at[tuple(place)].set(low).at[tuple(neighbour)].set(largest)


def block_scale(stream_key, shape, pieces, low, largest):
    level = 1.0
    for position, shards_of in pieces:
        draws = jax.random.uniform(jax.random.fold_in(jax.random.fold_in(stream_key, 6), position), (shards_of,), jnp.float32, low / len(pieces), largest / len(pieces))
        level = level * jnp.repeat(jnp.exp(draws), shape[position] // shards_of).reshape((-1,) + (1,) * (len(shape) - 1 - position))
    return level


def noise(own_key, dims, width, reach, split=(), kind=jnp.bfloat16):
    level = block_scale(own_key, dims, split, -0.22, 0.18) if split else 1.0
    array = jax.random.normal(own_key, dims, jnp.float32) * width * level
    return jnp.minimum(jnp.maximum(array, -reach), reach).astype(kind)


def setup_inputs(seed: int = 0) -> dict:
    arg_keys = jax.random.split(jax.random.key(seed), 5)
    return {
        "echoes": noise(arg_keys[0], (2, PULSES, CHANNELS, GATES), 1.0, 6.0, ((1, 8), (3, 4))),
        "chirp": noise(arg_keys[1], (2, TAPS), (2 * TAPS) ** -0.5, 0.1875),
        "ridge": draw_ridge(jax.random.fold_in(arg_keys[4], 71), 0),
        "counts": touch_ends(jax.random.randint(arg_keys[3], (PULSES,), 1, NBLK + 1), jax.random.fold_in(arg_keys[3], 1), 1, NBLK).astype(jnp.int32),
    }


LOADING = 0.1

def compress_channel(channel_data, chirp):
    signal = lax.complex(channel_data[0].astype(jnp.float32), channel_data[1].astype(jnp.float32))
    filter_taps = lax.complex(chirp[0].astype(jnp.float32), chirp[1].astype(jnp.float32))
    total_length = GATES + TAPS
    product = jnp.fft.fft(signal, n=total_length, axis=1) * jnp.fft.fft(filter_taps, n=total_length)[None, :]
    convolved = jnp.fft.ifft(product, axis=1)[:, :GATES]
    real_round = jnp.real(convolved).astype(jnp.bfloat16)
    imag_round = jnp.imag(convolved).astype(jnp.bfloat16)
    real_round, imag_round = lax.optimization_barrier((real_round, imag_round))
    rounded = lax.complex(real_round.astype(jnp.float32), imag_round.astype(jnp.float32))
    doppler = jnp.fft.fft(rounded, axis=0) / math.sqrt(PULSES)
    return jnp.stack([jnp.real(doppler), jnp.imag(doppler)], axis=1).astype(jnp.bfloat16)

def whiten_bin(operands):
    data, count, flag = operands
    values = data.astype(jnp.float32).reshape(2 * CHANNELS, N_RNG, GATE_DEV)
    block_index = jnp.arange(GATE_DEV, dtype=jnp.int32) // TRAIN_BLK
    training = (block_index < count).astype(jnp.float32)
    masked = values * training[None, None, :]
    rotated = jnp.concatenate([-masked[CHANNELS:], masked[:CHANNELS]], axis=0)
    paired = jnp.concatenate([masked, rotated], axis=2)
    grams = jnp.einsum('ksg,jsg->skj', paired, paired, precision=lax.Precision.HIGHEST)
    prefix = jnp.cumsum(grams, axis=0)
    used = ((jnp.arange(N_RNG, dtype=jnp.int32) + 1) * count * TRAIN_BLK).astype(jnp.float32)
    covariance = prefix / used[:, None, None]
    identity = jnp.eye(2 * CHANNELS, dtype=jnp.float32)
    loaded = jnp.where(flag == 1, covariance, covariance * identity[None]) + LOADING * identity[None]
    factor = jnp.linalg.cholesky(loaded)
    segments = jnp.moveaxis(values, 1, 0)
    solved = jax.scipy.linalg.solve_triangular(factor, segments, lower=True)
    return jnp.moveaxis(solved, 0, 1).reshape(2 * CHANNELS, GATES).astype(jnp.bfloat16)

def reference(echoes, chirp, ridge, counts):
    by_channel = jnp.moveaxis(echoes, 2, 0)
    cube = lax.map(lambda channel_data: compress_channel(channel_data, chirp), by_channel)
    spectra = jnp.transpose(cube, (1, 2, 0, 3)).reshape(PULSES, 2 * CHANNELS, GATES)
    return lax.map(whiten_bin, (spectra, counts, ridge))
```

```python
import functools
import math

import jax
import jax.numpy as jnp
import numpy as np
from jax import lax
from jax.experimental import pallas as pl
from jax.experimental.pallas import tpu as pltpu
from jax.sharding import PartitionSpec as P

TRAIN_BLK = 512
LOADING = 0.1
LANES = 128
WIDTH = 256
VMEM_LIMIT = 50 * 1024 * 1024

GATE_PLAN = (1, 6, 1)
BIN_PLAN = (4, 2, 1, 1)


def params():
    return pltpu.CompilerParams(vmem_limit_bytes=VMEM_LIMIT)


def cost(flops, nbytes):
    return pl.CostEstimate(flops=int(flops), bytes_accessed=int(nbytes), transcendentals=0)


def chunks(total, plan):
    unit = total // sum(plan)
    sizes = [unit * part for part in plan]
    starts = [sum(sizes[:k]) for k in range(len(sizes))]
    return list(zip(starts, sizes))


def table_kernel(taps, sequence_ref, table_ref):
    rows = taps + WIDTH
    length = sequence_ref.shape[1]
    tables = []
    for component in range(2):
        wide = jnp.broadcast_to(sequence_ref[component : component + 1, :], (rows, length))
        rolled = pltpu.roll(wide, 0, 1, stride=1, stride_axis=0)
        tables.append(rolled[:, :WIDTH])
    real, imag = tables
    table_ref[:rows, :WIDTH] = real.astype(table_ref.dtype)
    table_ref[:rows, WIDTH:] = imag.astype(table_ref.dtype)
    table_ref[rows:, :WIDTH] = (-imag).astype(table_ref.dtype)
    table_ref[rows:, WIDTH:] = real.astype(table_ref.dtype)


def filter_table(chirp):
    taps = chirp.shape[1]
    pad = taps + WIDTH - taps % WIDTH - WIDTH
    sequence = jnp.concatenate([jnp.zeros((2, pad), chirp.dtype), chirp], axis=1).astype(jnp.float32)
    return pl.pallas_call(
        functools.partial(table_kernel, taps),
        out_shape=jax.ShapeDtypeStruct((2 * (taps + WIDTH), 2 * WIDTH), chirp.dtype),
        compiler_params=params(),
        name="filter_table",
    )(sequence)


def compress_kernel(taps, has_halo, group, *refs):
    if has_halo:
        table_ref, halo_ref, before_ref, now_ref, out_ref, wide_ref = refs
    else:
        table_ref, before_ref, now_ref, out_ref, wide_ref = refs
    pulses, channels, gates = now_ref.shape[1:]
    rows = pulses * channels
    parts = []
    for component in range(2):
        before = before_ref[component]
        if has_halo:
            before = jnp.where(pl.program_id(1) == 0, halo_ref[component], before)
        parts.append(
            jnp.concatenate(
                [before.reshape(rows, taps), now_ref[component].reshape(rows, gates)], axis=1
            )
        )
    for tile in range(gates // WIDTH):
        first = tile * WIDTH
        window = jnp.concatenate([part[:, first : first + taps + WIDTH] for part in parts], axis=1)
        filtered = jnp.dot(window, table_ref[...], preferred_element_type=jnp.float32)
        per_part = WIDTH // LANES
        for lane_tile in range(2 * per_part):
            wide_ref[lane_tile] = filtered[:, lane_tile * LANES : (lane_tile + 1) * LANES]
        for channel in range(channels):
            for lane_tile in range(2 * per_part):
                component = lane_tile // per_part
                lanes = first + lane_tile % per_part * LANES
                piece = wide_ref[lane_tile, pl.ds(channel, pulses, stride=channels), :]
                out_ref[
                    channel // group,
                    channel % group,
                    component * pulses : (component + 1) * pulses,
                    lanes : lanes + LANES,
                ] = piece.astype(out_ref.dtype)


def compress(echoes, table, halo, start, size, groups):
    _, pulses, channels, gates = echoes.shape
    taps = table.shape[0] // 2 - WIDTH
    group = channels // groups
    at_once = max(16, group)
    step = taps
    offset = start // step
    has_halo = start == 0
    block = (2, pulses, at_once, step)
    in_specs = [pl.BlockSpec(table.shape, lambda c, g: (0, 0))]
    operands = [table]
    if has_halo:
        in_specs.append(pl.BlockSpec(block, lambda c, g: (0, 0, c, 0)))
        operands.append(halo)
    in_specs.append(pl.BlockSpec(block, lambda c, g: (0, 0, c, jnp.maximum(offset + g - 1, 0))))
    in_specs.append(pl.BlockSpec(block, lambda c, g: (0, 0, c, offset + g)))
    operands += [echoes, echoes]
    return pl.pallas_call(
        functools.partial(compress_kernel, taps, has_halo, group),
        grid=(channels // at_once, size // step),
        in_specs=in_specs,
        out_specs=pl.BlockSpec(
            (at_once // group, group, 2 * pulses, step), lambda c, g: (c, 0, 0, g)
        ),
        out_shape=jax.ShapeDtypeStruct((groups, group, 2 * pulses, size), echoes.dtype),
        scratch_shapes=[pltpu.VMEM((2 * WIDTH // LANES, pulses * at_once, LANES), jnp.float32)],
        compiler_params=params(),
        cost_estimate=cost(
            2 * pulses * channels * size * (taps + WIDTH) * 4, 12 * pulses * channels * size
        ),
        name="compress",
    )(*operands)


def doppler_tables(pulse_count, groups):
    index = np.arange(pulse_count, dtype=np.int64)
    angles = (index[:, None] * index[None, :] % pulse_count) * (2.0 * math.pi / pulse_count)
    cosine = np.cos(angles) / math.sqrt(pulse_count)
    sine = np.sin(angles) / math.sqrt(pulse_count)
    local = pulse_count // groups
    cosine = cosine.reshape(pulse_count, groups, 1, local)
    sine = sine.reshape(pulse_count, groups, 1, local)
    real_rows = np.concatenate([cosine, sine], axis=2).reshape(pulse_count, 2 * pulse_count)
    imag_rows = np.concatenate([-sine, cosine], axis=2).reshape(pulse_count, 2 * pulse_count)
    table = np.concatenate([real_rows, imag_rows], axis=0)
    high = table.astype(jnp.bfloat16)
    low = (table - high.astype(np.float64)).astype(jnp.bfloat16)
    return jnp.asarray(high), jnp.asarray(low)


def doppler_kernel(plan, carried, *refs):
    high_ref, low_ref, in_ref = refs[:3]
    outs = refs[3 + carried : 3 + carried + len(plan)]
    wide_ref = refs[-1]
    groups, group, depth, gates = in_ref.shape
    total = groups * depth
    bins = total // 2
    local = bins // groups
    for channel in range(group):
        data = in_ref[:, channel].reshape(total, gates)
        spectrum = jnp.dot(high_ref[...], data, preferred_element_type=jnp.float32)
        spectrum = spectrum + jnp.dot(low_ref[...], data, preferred_element_type=jnp.float32)
        for lane_tile in range(gates // LANES):
            wide_ref[lane_tile, channel * total : (channel + 1) * total, :] = spectrum[
                :, lane_tile * LANES : (lane_tile + 1) * LANES
            ]
    for out_ref, (first, count) in zip(outs, plan):
        for place in range(groups):

            def move(k, carry, out_ref=out_ref, base=place * local + first, place=place):
                for lane_tile in range(gates // LANES):
                    real = wide_ref[lane_tile, pl.ds(base + k, group, stride=total), :]
                    imag = wide_ref[lane_tile, pl.ds(base + k + bins, group, stride=total), :]
                    out_ref[place, k, :, lane_tile * LANES : (lane_tile + 1) * LANES] = (
                        jnp.concatenate([real, imag], axis=0).astype(out_ref.dtype)
                    )
                return carry

            lax.fori_loop(0, count, move, 0, unroll=True)


def doppler(received, tables, earlier, start, gates, plan):
    groups, group, depth, size = received.shape
    total = groups * depth
    step = WIDTH
    offset = start // step
    table_spec = pl.BlockSpec((total, total), lambda g: (0, 0))
    in_specs = [
        table_spec,
        table_spec,
        pl.BlockSpec((groups, group, depth, step), lambda g: (0, 0, 0, g)),
    ]
    operands = [*tables, received]
    aliases = {}
    if earlier is not None:
        for k, array in enumerate(earlier):
            aliases[len(operands)] = k
            operands.append(array)
            in_specs.append(pl.BlockSpec(memory_space=pl.ANY))
    return pl.pallas_call(
        functools.partial(doppler_kernel, plan, 0 if earlier is None else len(earlier)),
        grid=(size // step,),
        in_specs=in_specs,
        out_specs=[
            pl.BlockSpec((groups, count, 2 * group, step), lambda g: (0, 0, 0, offset + g))
            for _, count in plan
        ],
        out_shape=[
            jax.ShapeDtypeStruct((groups, count, 2 * group, gates), received.dtype)
            for _, count in plan
        ],
        scratch_shapes=[pltpu.VMEM((step // LANES, group * total, LANES), jnp.float32)],
        input_output_aliases=aliases,
        compiler_params=params(),
        cost_estimate=cost(4 * total * total * group * size, 4 * total * group * size),
        name="doppler",
    )(*operands)


def doppler_plain(received, tables, plan):
    groups, group, depth, size = received.shape
    total = groups * depth
    data = jnp.moveaxis(received, 1, 2).reshape(total, group * size)
    spectrum = jnp.dot(tables[0], data, preferred_element_type=jnp.float32)
    spectrum = spectrum + jnp.dot(tables[1], data, preferred_element_type=jnp.float32)
    spectrum = spectrum.astype(received.dtype).reshape(2, groups, depth // 2, group, size)
    spectrum = spectrum.transpose(1, 2, 0, 3, 4).reshape(groups, depth // 2, 2 * group, size)
    return [spectrum[:, first : first + count] for first, count in plan]


def natural_rows(matrix, groups):
    half = matrix.shape[0] // groups // 2
    pieces = [matrix[2 * half * s : 2 * half * s + half] for s in range(groups)]
    pieces += [matrix[2 * half * s + half : 2 * half * (s + 1)] for s in range(groups)]
    return jnp.concatenate(pieces, axis=0)


def grouped_rows(matrix, groups):
    rows = matrix.shape[0]
    half = rows // groups // 2
    pieces = []
    for s in range(groups):
        pieces.append(matrix[half * s : half * (s + 1)])
        pieces.append(matrix[rows // 2 + half * s : rows // 2 + half * (s + 1)])
    return jnp.concatenate(pieces, axis=0)


def gram_kernel(counts_ref, data_ref, out_ref, total_ref):
    groups, _, rows, gates = data_ref.shape
    size = groups * rows
    total_ref[...] = jnp.zeros_like(total_ref)
    count = counts_ref[pl.program_id(0)]
    for block in range(gates // TRAIN_BLK):

        @pl.when(block < count)
        def _():
            data = data_ref[:, 0, :, block * TRAIN_BLK : (block + 1) * TRAIN_BLK]
            data = data.reshape(size, TRAIN_BLK)
            total_ref[...] += lax.dot_general(
                data, data, (((1,), (1,)), ((), ())), preferred_element_type=jnp.float32
            )

    gram = natural_rows(natural_rows(total_ref[...], groups).T, groups)
    half = size // 2
    lane = lax.broadcasted_iota(jnp.int32, (half, size), 1)
    turned = pltpu.roll(gram[half:], half, 1)
    out_ref[0] = gram[:half] + jnp.where(lane < half, turned, -turned)


def gram(data, counts):
    groups, bins, rows, gates = data.shape
    size = groups * rows
    return pl.pallas_call(
        gram_kernel,
        grid_spec=pltpu.PrefetchScalarGridSpec(
            num_scalar_prefetch=1,
            grid=(bins,),
            in_specs=[pl.BlockSpec((groups, 1, rows, gates), lambda b, counts: (0, b, 0, 0))],
            out_specs=pl.BlockSpec((1, size // 2, size), lambda b, counts: (b, 0, 0)),
            scratch_shapes=[pltpu.VMEM((size, size), jnp.float32)],
        ),
        out_shape=jax.ShapeDtypeStruct((bins, size // 2, size), jnp.float32),
        compiler_params=params(),
        cost_estimate=cost(2 * bins * size * size * gates, 2 * bins * size * gates),
        name="gram",
    )(counts, data)


def factor_kernel(groups, segment_ref, counts_ref, ridge_ref, grams_ref, out_ref, work_ref, inverse_ref):
    segments, bins, half, size = grams_ref.shape
    segment = segment_ref[0]
    lane = lax.broadcasted_iota(jnp.int32, (half, size), 1)
    row = lax.broadcasted_iota(jnp.int32, (size, size), 0)
    column = lax.broadcasted_iota(jnp.int32, (size, size), 1)
    for b in range(bins):
        top = grams_ref[0, b]
        for t in range(1, segments):
            top = jnp.where(t <= segment, top + grams_ref[t, b], top)
        turned = pltpu.roll(top, half, 1)
        full = jnp.concatenate([top, jnp.where(lane < half, -turned, turned)], axis=0)
        used = ((segment + 1) * counts_ref[b] * TRAIN_BLK).astype(jnp.float32)
        covariance = full / used
        kept = jnp.logical_or(ridge_ref[b] == 1, row == column)
        work_ref[b] = jnp.where(kept, covariance, 0.0) + jnp.where(row == column, LOADING, 0.0)

    one_lane = lax.broadcasted_iota(jnp.int32, (1, size), 1)
    parts = 4
    for part in range(parts):
        low = part * size // parts
        lanes = lax.broadcasted_iota(jnp.int32, (size - low, size), 1)

        def step(j, carry, low=low, lanes=lanes):
            here = one_lane == j
            mask = lanes == j
            rows = [work_ref[b, pl.ds(j, 1), :] for b in range(bins)]
            pivots = [jnp.sum(jnp.where(here, row, 0.0), axis=1, keepdims=True) for row in rows]
            for b in range(bins):
                kept = jnp.where(one_lane < j, rows[b], jnp.where(here, 1.0, 0.0))
                inverse_ref[b, pl.ds(j, 1), :] = kept * lax.rsqrt(pivots[b])
            scaled = [jnp.where(here, 1.0, row) / pivot for row, pivot in zip(rows, pivots)]
            for b in range(bins):
                matrix = work_ref[b, low:, :]
                entries = jnp.sum(jnp.where(mask, matrix, 0.0), axis=1, keepdims=True)
                work_ref[b, low:, :] = jnp.where(mask, 0.0, matrix) - entries * scaled[b]
            return carry

        lax.fori_loop(low, low + size // parts, step, 0)
    for b in range(bins):
        inverse = grouped_rows(inverse_ref[b].T, groups).T
        high = inverse.astype(jnp.bfloat16)
        out_ref[b, :, :size] = high
        out_ref[b, :, size:] = (inverse - high.astype(jnp.float32)).astype(jnp.bfloat16)


def inverse_factors(grams, segment, counts, ridge, groups):
    segments, bins, half, size = grams.shape
    smem = pl.BlockSpec(memory_space=pltpu.SMEM)
    return pl.pallas_call(
        functools.partial(factor_kernel, groups),
        in_specs=[smem, smem, smem, pl.BlockSpec(memory_space=pltpu.VMEM)],
        out_specs=pl.BlockSpec(memory_space=pltpu.VMEM),
        out_shape=jax.ShapeDtypeStruct((bins, size, 2 * size), jnp.bfloat16),
        scratch_shapes=[
            pltpu.VMEM((bins, size, size), jnp.float32),
            pltpu.VMEM((bins, size, size), jnp.float32),
        ],
        compiler_params=params(),
        cost_estimate=cost(2 * bins * size**3 * 20, 4 * segments * bins * half * size),
        name="inverse_factors",
    )(segment, counts, ridge, grams)


def whiten_kernel(inverse_ref, data_ref, *refs):
    out_ref = refs[-1]
    groups, _, rows, gates = data_ref.shape
    size = groups * rows
    step = 1024 if gates % 1024 == 0 else gates
    for first in range(0, gates, step):
        data = data_ref[:, 0, :, first : first + step].reshape(size, step)
        twice = jnp.concatenate([data, data], axis=0)
        out_ref[0, :, first : first + step] = jnp.dot(
            inverse_ref[0], twice, preferred_element_type=jnp.float32
        ).astype(out_ref.dtype)


def whiten(inverse, data, earlier, first, total):
    groups, bins, rows, gates = data.shape
    size = groups * rows
    in_specs = [
        pl.BlockSpec((1, size, 2 * size), lambda b: (b, 0, 0)),
        pl.BlockSpec((groups, 1, rows, gates), lambda b: (0, b, 0, 0)),
    ]
    operands = [inverse, data]
    aliases = {}
    if earlier is not None:
        in_specs.append(pl.BlockSpec(memory_space=pl.ANY))
        operands.append(earlier)
        aliases = {2: 0}
    return pl.pallas_call(
        whiten_kernel,
        grid=(bins,),
        in_specs=in_specs,
        out_specs=pl.BlockSpec((1, size, gates), lambda b: (first + b, 0, 0)),
        out_shape=jax.ShapeDtypeStruct((total, size, gates), data.dtype),
        input_output_aliases=aliases,
        compiler_params=params(),
        cost_estimate=cost(4 * bins * size * size * gates, 4 * bins * size * gates),
        name="whiten",
    )(*operands)


def exchange(array):
    return lax.all_to_all(array, "dop", split_axis=0, concat_axis=0, tiled=True)


def per_device(echoes, chirp, ridge, counts):
    taps = chirp.shape[1]
    _, pulses, channels, gates = echoes.shape
    groups = lax.axis_size("dop")
    group = channels // groups
    pulse_count = pulses * groups
    bins = counts.shape[0]
    bin_plan = chunks(bins, BIN_PLAN)
    gate_plan = [(gates - start - size, size) for start, size in chunks(gates, GATE_PLAN)]

    segments = lax.axis_size("rng")
    route = [(k, k + 1) for k in range(segments - 1)]
    halo = lax.ppermute(echoes[:, :, :, gates - taps :], "rng", route)
    table = filter_table(chirp)
    tables = doppler_tables(pulse_count, groups)

    received = []
    for start, size in gate_plan:
        received.append(exchange(compress(echoes, table, halo, start, size, groups)))

    if group % 8 == 0:
        spectra = None
        for (start, size), part in zip(gate_plan, received):
            spectra = doppler(part, tables, spectra, start, gates, bin_plan)
    else:
        pieces = [doppler_plain(part, tables, bin_plan) for part in received]
        spectra = [jnp.concatenate(piece[::-1], axis=3) for piece in zip(*pieces)]

    segment = lax.axis_index("rng").reshape(1)
    whitened = None
    data = exchange(spectra[0])
    for k, (first, count) in enumerate(bin_plan):
        if k + 1 < len(bin_plan):
            if whitened is None:
                following, data = lax.optimization_barrier((spectra[k + 1], data))
            else:
                following, data, whitened = lax.optimization_barrier(
                    (spectra[k + 1], data, whitened)
                )
            following = exchange(following)
        if group % 8:
            data = data.reshape(groups, count, 2, group, gates).transpose(1, 2, 0, 3, 4)
            data = data.reshape(1, count, 2 * channels, gates)
        these = counts[first : first + count]
        grams = lax.all_gather(gram(data, these), "rng")
        inverse = inverse_factors(
            grams, segment, these, ridge[first : first + count], data.shape[0]
        )
        whitened = whiten(inverse, data, whitened, first, bins)
        data = following
    return whitened


def solution(mesh):
    in_specs = (P(None, "dop", None, "rng"), P(), P("dop"), P("dop"))
    out_specs = P("dop", None, "rng")
    return jax.shard_map(
        per_device, mesh=mesh, in_specs=in_specs, out_specs=out_specs, check_vma=False
    )
```

```python
import functools
import math

import jax
import jax.numpy as jnp
import numpy as np
from jax import lax
from jax.experimental import pallas as pl
from jax.experimental.pallas import tpu as pltpu
from jax.sharding import PartitionSpec as P

TRAIN_BLK = 512
LOADING = 0.1
LANES = 128
WIDTH = 256
VMEM_LIMIT = 50 * 1024 * 1024

GATE_PLAN = (1, 6, 1)
BIN_PLAN = (12, 3, 1)


def params():
    return pltpu.CompilerParams(vmem_limit_bytes=VMEM_LIMIT)


def cost(flops, nbytes):
    return pl.CostEstimate(flops=int(flops), bytes_accessed=int(nbytes), transcendentals=0)


def chunks(total, plan):
    sizes = [max(1, total * part // sum(plan)) for part in plan]
    sizes[0] = total - sum(sizes[1:])
    starts = [sum(sizes[:k]) for k in range(len(sizes))]
    return list(zip(starts, sizes))


def table_kernel(taps, sequence_ref, table_ref):
    rows = taps + WIDTH
    length = sequence_ref.shape[1]
    tables = []
    for component in range(2):
        wide = jnp.broadcast_to(sequence_ref[component : component + 1, :], (rows, length))
        rolled = pltpu.roll(wide, 0, 1, stride=1, stride_axis=0)
        tables.append(rolled[:, :WIDTH])
    real, imag = tables
    table_ref[:rows, :WIDTH] = real.astype(table_ref.dtype)
    table_ref[:rows, WIDTH:] = imag.astype(table_ref.dtype)
    table_ref[rows:, :WIDTH] = (-imag).astype(table_ref.dtype)
    table_ref[rows:, WIDTH:] = real.astype(table_ref.dtype)


def filter_table(chirp):
    taps = chirp.shape[1]
    pad = taps + WIDTH - taps % WIDTH - WIDTH
    sequence = jnp.concatenate([jnp.zeros((2, pad), chirp.dtype), chirp], axis=1).astype(jnp.float32)
    return pl.pallas_call(
        functools.partial(table_kernel, taps),
        out_shape=jax.ShapeDtypeStruct((2 * (taps + WIDTH), 2 * WIDTH), chirp.dtype),
        compiler_params=params(),
        name="filter_table",
    )(sequence)


def compress_kernel(taps, has_halo, group, *refs):
    if has_halo:
        table_ref, halo_ref, before_ref, now_ref, out_ref, wide_ref = refs
    else:
        table_ref, before_ref, now_ref, out_ref, wide_ref = refs
    pulses, channels, gates = now_ref.shape[1:]
    rows = pulses * channels
    parts = []
    for component in range(2):
        before = before_ref[component]
        if has_halo:
            before = jnp.where(pl.program_id(1) == 0, halo_ref[component], before)
        parts.append(
            jnp.concatenate(
                [before.reshape(rows, taps), now_ref[component].reshape(rows, gates)], axis=1
            )
        )
    for tile in range(gates // WIDTH):
        first = tile * WIDTH
        window = jnp.concatenate([part[:, first : first + taps + WIDTH] for part in parts], axis=1)
        filtered = jnp.dot(window, table_ref[...], preferred_element_type=jnp.float32)
        per_part = WIDTH // LANES
        for lane_tile in range(2 * per_part):
            wide_ref[lane_tile] = filtered[:, lane_tile * LANES : (lane_tile + 1) * LANES]
        for channel in range(channels):
            for lane_tile in range(2 * per_part):
                component = lane_tile // per_part
                lanes = first + lane_tile % per_part * LANES
                piece = wide_ref[lane_tile, pl.ds(channel, pulses, stride=channels), :]
                out_ref[
                    channel // group,
                    channel % group,
                    component * pulses : (component + 1) * pulses,
                    lanes : lanes + LANES,
                ] = piece.astype(out_ref.dtype)


def compress(echoes, table, halo, start, size, groups):
    _, pulses, channels, gates = echoes.shape
    taps = table.shape[0] // 2 - WIDTH
    group = channels // groups
    at_once = max(16, group)
    step = taps
    offset = start // step
    has_halo = start == 0
    block = (2, pulses, at_once, step)
    in_specs = [pl.BlockSpec(table.shape, lambda c, g: (0, 0))]
    operands = [table]
    if has_halo:
        in_specs.append(pl.BlockSpec(block, lambda c, g: (0, 0, c, 0)))
        operands.append(halo)
    in_specs.append(pl.BlockSpec(block, lambda c, g: (0, 0, c, jnp.maximum(offset + g - 1, 0))))
    in_specs.append(pl.BlockSpec(block, lambda c, g: (0, 0, c, offset + g)))
    operands += [echoes, echoes]
    return pl.pallas_call(
        functools.partial(compress_kernel, taps, has_halo, group),
        grid=(channels // at_once, size // step),
        in_specs=in_specs,
        out_specs=pl.BlockSpec(
            (at_once // group, group, 2 * pulses, step), lambda c, g: (c, 0, 0, g)
        ),
        out_shape=jax.ShapeDtypeStruct((groups, group, 2 * pulses, size), echoes.dtype),
        scratch_shapes=[pltpu.VMEM((2 * WIDTH // LANES, pulses * at_once, LANES), jnp.float32)],
        compiler_params=params(),
        cost_estimate=cost(
            2 * pulses * channels * size * (taps + WIDTH) * 4, 12 * pulses * channels * size
        ),
        name="compress",
    )(*operands)


def doppler_tables(pulse_count, groups):
    index = np.arange(pulse_count, dtype=np.int64)
    angles = (index[:, None] * index[None, :] % pulse_count) * (2.0 * math.pi / pulse_count)
    cosine = np.cos(angles) / math.sqrt(pulse_count)
    sine = np.sin(angles) / math.sqrt(pulse_count)
    local = pulse_count // groups
    cosine = cosine.reshape(pulse_count, groups, 1, local)
    sine = sine.reshape(pulse_count, groups, 1, local)
    real_rows = np.concatenate([cosine, sine], axis=2).reshape(pulse_count, 2 * pulse_count)
    imag_rows = np.concatenate([-sine, cosine], axis=2).reshape(pulse_count, 2 * pulse_count)
    table = np.concatenate([real_rows, imag_rows], axis=0)
    high = table.astype(jnp.bfloat16)
    low = (table - high.astype(np.float64)).astype(jnp.bfloat16)
    return jnp.asarray(high), jnp.asarray(low)


def doppler_kernel(plan, carried, *refs):
    high_ref, low_ref, in_ref = refs[:3]
    outs = refs[3 + carried : 3 + carried + len(plan)]
    wide_ref = refs[-1]
    groups, group, depth, gates = in_ref.shape
    total = groups * depth
    bins = total // 2
    local = bins // groups
    for channel in range(group):
        data = in_ref[:, channel].reshape(total, gates)
        spectrum = jnp.dot(high_ref[...], data, preferred_element_type=jnp.float32)
        spectrum = spectrum + jnp.dot(low_ref[...], data, preferred_element_type=jnp.float32)
        for lane_tile in range(gates // LANES):
            wide_ref[lane_tile, pl.ds(channel, total, stride=group), :] = spectrum[
                :, lane_tile * LANES : (lane_tile + 1) * LANES
            ]
    for out_ref, (first, count) in zip(outs, plan):
        for place in range(groups):

            def move(k, carry, out_ref=out_ref, base=place * local + first, place=place):
                for lane_tile in range(gates // LANES):
                    real = wide_ref[lane_tile, pl.ds((base + k) * group, group), :]
                    imag = wide_ref[lane_tile, pl.ds((base + k + bins) * group, group), :]
                    out_ref[place, k, :, lane_tile * LANES : (lane_tile + 1) * LANES] = (
                        jnp.concatenate([real, imag], axis=0).astype(out_ref.dtype)
                    )
                return carry

            lax.fori_loop(0, count, move, 0, unroll=True)


def doppler(received, tables, earlier, start, gates, plan):
    groups, group, depth, size = received.shape
    total = groups * depth
    step = WIDTH
    offset = start // step
    table_spec = pl.BlockSpec((total, total), lambda g: (0, 0))
    in_specs = [
        table_spec,
        table_spec,
        pl.BlockSpec((groups, group, depth, step), lambda g: (0, 0, 0, g)),
    ]
    operands = [*tables, received]
    aliases = {}
    if earlier is not None:
        for k, array in enumerate(earlier):
            aliases[len(operands)] = k
            operands.append(array)
            in_specs.append(pl.BlockSpec(memory_space=pl.ANY))
    return pl.pallas_call(
        functools.partial(doppler_kernel, plan, 0 if earlier is None else len(earlier)),
        grid=(size // step,),
        in_specs=in_specs,
        out_specs=[
            pl.BlockSpec((groups, count, 2 * group, step), lambda g: (0, 0, 0, offset + g))
            for _, count in plan
        ],
        out_shape=[
            jax.ShapeDtypeStruct((groups, count, 2 * group, gates), received.dtype)
            for _, count in plan
        ],
        scratch_shapes=[pltpu.VMEM((step // LANES, group * total, LANES), jnp.float32)],
        input_output_aliases=aliases,
        compiler_params=params(),
        cost_estimate=cost(4 * total * total * group * size, 4 * total * group * size),
        name="doppler",
    )(*operands)


def doppler_plain(received, tables, plan):
    groups, group, depth, size = received.shape
    total = groups * depth
    data = jnp.moveaxis(received, 1, 2).reshape(total, group * size)
    spectrum = jnp.dot(tables[0], data, preferred_element_type=jnp.float32)
    spectrum = spectrum + jnp.dot(tables[1], data, preferred_element_type=jnp.float32)
    spectrum = spectrum.astype(received.dtype).reshape(2, groups, depth // 2, group, size)
    spectrum = spectrum.transpose(1, 2, 0, 3, 4).reshape(groups, depth // 2, 2 * group, size)
    return [spectrum[:, first : first + count] for first, count in plan]


def natural_rows(matrix, groups):
    half = matrix.shape[0] // groups // 2
    pieces = [matrix[2 * half * s : 2 * half * s + half] for s in range(groups)]
    pieces += [matrix[2 * half * s + half : 2 * half * (s + 1)] for s in range(groups)]
    return jnp.concatenate(pieces, axis=0)


def grouped_rows(matrix, groups):
    rows = matrix.shape[0]
    half = rows // groups // 2
    pieces = []
    for s in range(groups):
        pieces.append(matrix[half * s : half * (s + 1)])
        pieces.append(matrix[rows // 2 + half * s : rows // 2 + half * (s + 1)])
    return jnp.concatenate(pieces, axis=0)


def gram_kernel(counts_ref, data_ref, out_ref, total_ref):
    groups, _, rows, gates = data_ref.shape
    size = groups * rows
    total_ref[...] = jnp.zeros_like(total_ref)
    count = counts_ref[pl.program_id(0)]
    for block in range(gates // TRAIN_BLK):

        @pl.when(block < count)
        def _():
            data = data_ref[:, 0, :, block * TRAIN_BLK : (block + 1) * TRAIN_BLK]
            data = data.reshape(size, TRAIN_BLK)
            total_ref[...] += lax.dot_general(
                data, data, (((1,), (1,)), ((), ())), preferred_element_type=jnp.float32
            )

    gram = natural_rows(natural_rows(total_ref[...], groups).T, groups)
    half = size // 2
    lane = lax.broadcasted_iota(jnp.int32, (half, size), 1)
    turned = pltpu.roll(gram[half:], half, 1)
    out_ref[0] = gram[:half] + jnp.where(lane < half, turned, -turned)


def gram(data, counts):
    groups, bins, rows, gates = data.shape
    size = groups * rows
    return pl.pallas_call(
        gram_kernel,
        grid_spec=pltpu.PrefetchScalarGridSpec(
            num_scalar_prefetch=1,
            grid=(bins,),
            in_specs=[pl.BlockSpec((groups, 1, rows, gates), lambda b, counts: (0, b, 0, 0))],
            out_specs=pl.BlockSpec((1, size // 2, size), lambda b, counts: (b, 0, 0)),
            scratch_shapes=[pltpu.VMEM((size, size), jnp.float32)],
        ),
        out_shape=jax.ShapeDtypeStruct((bins, size // 2, size), jnp.float32),
        compiler_params=params(),
        cost_estimate=cost(2 * bins * size * size * gates, 2 * bins * size * gates),
        name="gram",
    )(counts, data)


def factor_kernel(groups, segment_ref, counts_ref, ridge_ref, grams_ref, out_ref, work_ref, inverse_ref):
    segments, bins, half, size = grams_ref.shape
    segment = segment_ref[0]
    lane = lax.broadcasted_iota(jnp.int32, (half, size), 1)
    row = lax.broadcasted_iota(jnp.int32, (size, size), 0)
    column = lax.broadcasted_iota(jnp.int32, (size, size), 1)
    for b in range(bins):
        top = grams_ref[0, b]
        for t in range(1, segments):
            top = jnp.where(t <= segment, top + grams_ref[t, b], top)
        turned = pltpu.roll(top, half, 1)
        full = jnp.concatenate([top, jnp.where(lane < half, -turned, turned)], axis=0)
        used = ((segment + 1) * counts_ref[b] * TRAIN_BLK).astype(jnp.float32)
        covariance = full / used
        kept = jnp.logical_or(ridge_ref[b] == 1, row == column)
        work_ref[b] = jnp.where(kept, covariance, 0.0) + jnp.where(row == column, LOADING, 0.0)

    one_lane = lax.broadcasted_iota(jnp.int32, (1, size), 1)
    parts = 4
    for part in range(parts):
        low = part * size // parts
        lanes = lax.broadcasted_iota(jnp.int32, (size - low, size), 1)

        def step(j, carry, low=low, lanes=lanes):
            here = one_lane == j
            mask = lanes == j
            rows = [work_ref[b, pl.ds(j, 1), :] for b in range(bins)]
            pivots = [jnp.sum(jnp.where(here, row, 0.0), axis=1, keepdims=True) for row in rows]
            for b in range(bins):
                kept = jnp.where(one_lane < j, rows[b], jnp.where(here, 1.0, 0.0))
                inverse_ref[b, pl.ds(j, 1), :] = kept * lax.rsqrt(pivots[b])
            scaled = [jnp.where(here, 1.0, row) / pivot for row, pivot in zip(rows, pivots)]
            for b in range(bins):
                matrix = work_ref[b, low:, :]
                entries = jnp.sum(jnp.where(mask, matrix, 0.0), axis=1, keepdims=True)
                work_ref[b, low:, :] = jnp.where(mask, 0.0, matrix) - entries * scaled[b]
            return carry

        lax.fori_loop(low, low + size // parts, step, 0)
    for b in range(bins):
        inverse = grouped_rows(inverse_ref[b].T, groups).T
        high = inverse.astype(jnp.bfloat16)
        out_ref[b, :, :size] = high
        out_ref[b, :, size:] = (inverse - high.astype(jnp.float32)).astype(jnp.bfloat16)


def inverse_factors(grams, segment, counts, ridge, groups):
    segments, bins, half, size = grams.shape
    smem = pl.BlockSpec(memory_space=pltpu.SMEM)
    return pl.pallas_call(
        functools.partial(factor_kernel, groups),
        in_specs=[smem, smem, smem, pl.BlockSpec(memory_space=pltpu.VMEM)],
        out_specs=pl.BlockSpec(memory_space=pltpu.VMEM),
        out_shape=jax.ShapeDtypeStruct((bins, size, 2 * size), jnp.bfloat16),
        scratch_shapes=[
            pltpu.VMEM((bins, size, size), jnp.float32),
            pltpu.VMEM((bins, size, size), jnp.float32),
        ],
        compiler_params=params(),
        cost_estimate=cost(2 * bins * size**3 * 20, 4 * segments * bins * half * size),
        name="inverse_factors",
    )(segment, counts, ridge, grams)


def whiten_kernel(inverse_ref, data_ref, *refs):
    out_ref = refs[-1]
    groups, _, rows, gates = data_ref.shape
    size = groups * rows
    step = 1024 if gates % 1024 == 0 else gates
    for first in range(0, gates, step):
        data = data_ref[:, 0, :, first : first + step].reshape(size, step)
        twice = jnp.concatenate([data, data], axis=0)
        out_ref[0, :, first : first + step] = jnp.dot(
            inverse_ref[0], twice, preferred_element_type=jnp.float32
        ).astype(out_ref.dtype)


def whiten(inverse, data, earlier, first, total):
    groups, bins, rows, gates = data.shape
    size = groups * rows
    in_specs = [
        pl.BlockSpec((1, size, 2 * size), lambda b: (b, 0, 0)),
        pl.BlockSpec((groups, 1, rows, gates), lambda b: (0, b, 0, 0)),
    ]
    operands = [inverse, data]
    aliases = {}
    if earlier is not None:
        in_specs.append(pl.BlockSpec(memory_space=pl.ANY))
        operands.append(earlier)
        aliases = {2: 0}
    return pl.pallas_call(
        whiten_kernel,
        grid=(bins,),
        in_specs=in_specs,
        out_specs=pl.BlockSpec((1, size, gates), lambda b: (first + b, 0, 0)),
        out_shape=jax.ShapeDtypeStruct((total, size, gates), data.dtype),
        input_output_aliases=aliases,
        compiler_params=params(),
        cost_estimate=cost(4 * bins * size * size * gates, 4 * bins * size * gates),
        name="whiten",
    )(*operands)


def exchange(array):
    return lax.all_to_all(array, "dop", split_axis=0, concat_axis=0, tiled=True)


def per_device(echoes, chirp, ridge, counts):
    taps = chirp.shape[1]
    _, pulses, channels, gates = echoes.shape
    groups = lax.axis_size("dop")
    group = channels // groups
    pulse_count = pulses * groups
    bins = counts.shape[0]
    bin_plan = chunks(bins, BIN_PLAN)
    gate_plan = [
        (gates - taps * (start + size), taps * size)
        for start, size in chunks(gates // taps, GATE_PLAN)
    ]

    segments = lax.axis_size("rng")
    route = [(k, k + 1) for k in range(segments - 1)]
    halo = lax.ppermute(echoes[:, :, :, gates - taps :], "rng", route)
    table = filter_table(chirp)
    tables = doppler_tables(pulse_count, groups)

    received = []
    for start, size in gate_plan:
        received.append(exchange(compress(echoes, table, halo, start, size, groups)))

    if group % 8 == 0:
        spectra = None
        for (start, size), part in zip(gate_plan, received):
            spectra = doppler(part, tables, spectra, start, gates, bin_plan)
    else:
        pieces = [doppler_plain(part, tables, bin_plan) for part in received]
        spectra = [jnp.concatenate(piece[::-1], axis=3) for piece in zip(*pieces)]

    segment = lax.axis_index("rng").reshape(1)
    whitened = None
    data = exchange(spectra[0])
    for k, (first, count) in enumerate(bin_plan):
        if k + 1 < len(bin_plan):
            if whitened is None:
                following, data = lax.optimization_barrier((spectra[k + 1], data))
            else:
                following, data, whitened = lax.optimization_barrier(
                    (spectra[k + 1], data, whitened)
                )
            following = exchange(following)
        if group % 8:
            data = data.reshape(groups, count, 2, group, gates).transpose(1, 2, 0, 3, 4)
            data = data.reshape(1, count, 2 * channels, gates)
        these = counts[first : first + count]
        grams = lax.all_gather(gram(data, these), "rng")
        inverse = inverse_factors(
            grams, segment, these, ridge[first : first + count], data.shape[0]
        )
        whitened = whiten(inverse, data, whitened, first, bins)
        data = following
    return whitened


def solution(mesh):
    in_specs = (P(None, "dop", None, "rng"), P(), P("dop"), P("dop"))
    out_specs = P("dop", None, "rng")
    return jax.shard_map(
        per_device, mesh=mesh, in_specs=in_specs, out_specs=out_specs, check_vma=False
    )
```

```python
import functools
import math

import jax
import jax.numpy as jnp
import numpy as np
from jax import lax
from jax.experimental import pallas as pl
from jax.experimental.pallas import tpu as pltpu
from jax.sharding import PartitionSpec as P

TRAIN_BLK = 512
LOADING = 0.1
LANES = 128
BINS_AT_ONCE = 4
PANEL = 16
WIDTH = 256
VMEM_LIMIT = 50 * 1024 * 1024

GATE_PLAN = (1, 6, 1)
BIN_PLAN = (12, 3, 1)


def params():
    return pltpu.CompilerParams(vmem_limit_bytes=VMEM_LIMIT)


def cost(flops, nbytes):
    return pl.CostEstimate(flops=int(flops), bytes_accessed=int(nbytes), transcendentals=0)


def chunks(total, plan):
    sizes = [max(1, total * part // sum(plan)) for part in plan]
    sizes[0] = total - sum(sizes[1:])
    starts = [sum(sizes[:k]) for k in range(len(sizes))]
    return list(zip(starts, sizes))


def table_kernel(taps, sequence_ref, table_ref):
    rows = taps + WIDTH
    length = sequence_ref.shape[1]
    tables = []
    for component in range(2):
        wide = jnp.broadcast_to(sequence_ref[component : component + 1, :], (rows, length))
        rolled = pltpu.roll(wide, 0, 1, stride=1, stride_axis=0)
        tables.append(rolled[:, :WIDTH])
    real, imag = tables
    table_ref[:rows, :WIDTH] = real.astype(table_ref.dtype)
    table_ref[:rows, WIDTH:] = imag.astype(table_ref.dtype)
    table_ref[rows:, :WIDTH] = (-imag).astype(table_ref.dtype)
    table_ref[rows:, WIDTH:] = real.astype(table_ref.dtype)


def filter_table(chirp):
    taps = chirp.shape[1]
    pad = taps + WIDTH - taps % WIDTH - WIDTH
    sequence = jnp.concatenate([jnp.zeros((2, pad), chirp.dtype), chirp], axis=1).astype(jnp.float32)
    return pl.pallas_call(
        functools.partial(table_kernel, taps),
        out_shape=jax.ShapeDtypeStruct((2 * (taps + WIDTH), 2 * WIDTH), chirp.dtype),
        compiler_params=params(),
        name="filter_table",
    )(sequence)


def compress_kernel(taps, has_halo, group, *refs):
    if has_halo:
        table_ref, halo_ref, before_ref, now_ref, out_ref, wide_ref = refs
    else:
        table_ref, before_ref, now_ref, out_ref, wide_ref = refs
    pulses, channels, gates = now_ref.shape[1:]
    rows = pulses * channels
    parts = []
    for component in range(2):
        before = before_ref[component]
        if has_halo:
            before = jnp.where(pl.program_id(1) == 0, halo_ref[component], before)
        parts.append(
            jnp.concatenate(
                [before.reshape(rows, taps), now_ref[component].reshape(rows, gates)], axis=1
            )
        )
    for tile in range(gates // WIDTH):
        first = tile * WIDTH
        window = jnp.concatenate([part[:, first : first + taps + WIDTH] for part in parts], axis=1)
        filtered = jnp.dot(window, table_ref[...], preferred_element_type=jnp.float32)
        per_part = WIDTH // LANES
        for lane_tile in range(2 * per_part):
            wide_ref[lane_tile] = filtered[:, lane_tile * LANES : (lane_tile + 1) * LANES]
        for channel in range(channels):
            for lane_tile in range(2 * per_part):
                component = lane_tile // per_part
                lanes = first + lane_tile % per_part * LANES
                piece = wide_ref[lane_tile, pl.ds(channel, pulses, stride=channels), :]
                out_ref[
                    channel // group,
                    channel % group,
                    component * pulses : (component + 1) * pulses,
                    lanes : lanes + LANES,
                ] = piece.astype(out_ref.dtype)


def compress(echoes, table, halo, start, size, groups):
    _, pulses, channels, gates = echoes.shape
    taps = table.shape[0] // 2 - WIDTH
    group = channels // groups
    at_once = max(16, group)
    step = taps
    offset = start // step
    has_halo = start == 0
    block = (2, pulses, at_once, step)
    in_specs = [pl.BlockSpec(table.shape, lambda c, g: (0, 0))]
    operands = [table]
    if has_halo:
        in_specs.append(pl.BlockSpec(block, lambda c, g: (0, 0, c, 0)))
        operands.append(halo)
    in_specs.append(pl.BlockSpec(block, lambda c, g: (0, 0, c, jnp.maximum(offset + g - 1, 0))))
    in_specs.append(pl.BlockSpec(block, lambda c, g: (0, 0, c, offset + g)))
    operands += [echoes, echoes]
    return pl.pallas_call(
        functools.partial(compress_kernel, taps, has_halo, group),
        grid=(channels // at_once, size // step),
        in_specs=in_specs,
        out_specs=pl.BlockSpec(
            (at_once // group, group, 2 * pulses, step), lambda c, g: (c, 0, 0, g)
        ),
        out_shape=jax.ShapeDtypeStruct((groups, group, 2 * pulses, size), echoes.dtype),
        scratch_shapes=[pltpu.VMEM((2 * WIDTH // LANES, pulses * at_once, LANES), jnp.float32)],
        compiler_params=params(),
        cost_estimate=cost(
            2 * pulses * channels * size * (taps + WIDTH) * 4, 12 * pulses * channels * size
        ),
        name="compress",
    )(*operands)


def doppler_tables(pulse_count, groups):
    index = np.arange(pulse_count, dtype=np.int64)
    angles = (index[:, None] * index[None, :] % pulse_count) * (2.0 * math.pi / pulse_count)
    cosine = np.cos(angles) / math.sqrt(pulse_count)
    sine = np.sin(angles) / math.sqrt(pulse_count)
    local = pulse_count // groups
    cosine = cosine.reshape(pulse_count, groups, 1, local)
    sine = sine.reshape(pulse_count, groups, 1, local)
    real_rows = np.concatenate([cosine, sine], axis=2).reshape(pulse_count, 2 * pulse_count)
    imag_rows = np.concatenate([-sine, cosine], axis=2).reshape(pulse_count, 2 * pulse_count)
    table = np.concatenate([real_rows, imag_rows], axis=0)
    high = table.astype(jnp.bfloat16)
    low = (table - high.astype(np.float64)).astype(jnp.bfloat16)
    return jnp.asarray(high), jnp.asarray(low)


def doppler_kernel(plan, carried, *refs):
    high_ref, low_ref, in_ref = refs[:3]
    outs = refs[3 + carried : 3 + carried + len(plan)]
    wide_ref = refs[-1]
    groups, group, depth, gates = in_ref.shape
    total = groups * depth
    bins = total // 2
    local = bins // groups
    for channel in range(group):
        data = in_ref[:, channel].reshape(total, gates)
        spectrum = jnp.dot(high_ref[...], data, preferred_element_type=jnp.float32)
        spectrum = spectrum + jnp.dot(low_ref[...], data, preferred_element_type=jnp.float32)
        for lane_tile in range(gates // LANES):
            wide_ref[lane_tile, pl.ds(channel, total, stride=group), :] = spectrum[
                :, lane_tile * LANES : (lane_tile + 1) * LANES
            ]
    for out_ref, (first, count) in zip(outs, plan):
        for place in range(groups):

            def move(k, carry, out_ref=out_ref, base=place * local + first, place=place):
                for lane_tile in range(gates // LANES):
                    real = wide_ref[lane_tile, pl.ds((base + k) * group, group), :]
                    imag = wide_ref[lane_tile, pl.ds((base + k + bins) * group, group), :]
                    out_ref[place, k, :, lane_tile * LANES : (lane_tile + 1) * LANES] = (
                        jnp.concatenate([real, imag], axis=0).astype(out_ref.dtype)
                    )
                return carry

            lax.fori_loop(0, count, move, 0, unroll=True)


def doppler(received, tables, earlier, start, gates, plan):
    groups, group, depth, size = received.shape
    total = groups * depth
    step = WIDTH
    offset = start // step
    table_spec = pl.BlockSpec((total, total), lambda g: (0, 0))
    in_specs = [
        table_spec,
        table_spec,
        pl.BlockSpec((groups, group, depth, step), lambda g: (0, 0, 0, g)),
    ]
    operands = [*tables, received]
    aliases = {}
    if earlier is not None:
        for k, array in enumerate(earlier):
            aliases[len(operands)] = k
            operands.append(array)
            in_specs.append(pl.BlockSpec(memory_space=pl.ANY))
    return pl.pallas_call(
        functools.partial(doppler_kernel, plan, 0 if earlier is None else len(earlier)),
        grid=(size // step,),
        in_specs=in_specs,
        out_specs=[
            pl.BlockSpec((groups, count, 2 * group, step), lambda g: (0, 0, 0, offset + g))
            for _, count in plan
        ],
        out_shape=[
            jax.ShapeDtypeStruct((groups, count, 2 * group, gates), received.dtype)
            for _, count in plan
        ],
        scratch_shapes=[pltpu.VMEM((step // LANES, group * total, LANES), jnp.float32)],
        input_output_aliases=aliases,
        compiler_params=params(),
        cost_estimate=cost(4 * total * total * group * size, 4 * total * group * size),
        name="doppler",
    )(*operands)


def doppler_plain(received, tables, plan):
    groups, group, depth, size = received.shape
    total = groups * depth
    data = jnp.moveaxis(received, 1, 2).reshape(total, group * size)
    spectrum = jnp.dot(tables[0], data, preferred_element_type=jnp.float32)
    spectrum = spectrum + jnp.dot(tables[1], data, preferred_element_type=jnp.float32)
    spectrum = spectrum.astype(received.dtype).reshape(2, groups, depth // 2, group, size)
    spectrum = spectrum.transpose(1, 2, 0, 3, 4).reshape(groups, depth // 2, 2 * group, size)
    return [spectrum[:, first : first + count] for first, count in plan]


def natural_rows(matrix, groups):
    half = matrix.shape[0] // groups // 2
    pieces = [matrix[2 * half * s : 2 * half * s + half] for s in range(groups)]
    pieces += [matrix[2 * half * s + half : 2 * half * (s + 1)] for s in range(groups)]
    return jnp.concatenate(pieces, axis=0)


def grouped_rows(matrix, groups):
    rows = matrix.shape[0]
    half = rows // groups // 2
    pieces = []
    for s in range(groups):
        pieces.append(matrix[half * s : half * (s + 1)])
        pieces.append(matrix[rows // 2 + half * s : rows // 2 + half * (s + 1)])
    return jnp.concatenate(pieces, axis=0)


def gram_kernel(counts_ref, data_ref, out_ref):
    groups, bins, rows, gates = data_ref.shape
    size = groups * rows
    half, quarter = size // 2, size // 4
    row = lax.broadcasted_iota(jnp.int32, (half, size), 0)
    lane = lax.broadcasted_iota(jnp.int32, (half, size), 1)
    gate = lax.broadcasted_iota(jnp.int32, (size, gates), 1)
    for b in range(bins):
        training = counts_ref[pl.program_id(0) * bins + b] * TRAIN_BLK
        data = data_ref[:, b].reshape(size, gates)
        data = jnp.where(gate < training, data, jnp.zeros_like(data))
        gram = lax.dot_general(
            data, data, (((1,), (1,)), ((), ())), preferred_element_type=jnp.float32
        )
        gram = natural_rows(natural_rows(gram, groups).T, groups)
        turned = pltpu.roll(gram[half:], half, 1)
        top = gram[:half] + jnp.where(lane < half, turned, -turned)
        packed = jnp.where(row >= lane, top, pltpu.roll(top, half, 1))
        out_ref[b] = jnp.where(
            lane[:quarter] < half, packed[:quarter], pltpu.roll(packed[quarter:], half, 1)
        )


def per_step(bins):
    return next(k for k in (BINS_AT_ONCE, 2, 1) if bins % k == 0)


def gram(data, counts):
    groups, bins, rows, gates = data.shape
    size = groups * rows
    at_once = per_step(bins)
    return pl.pallas_call(
        gram_kernel,
        grid_spec=pltpu.PrefetchScalarGridSpec(
            num_scalar_prefetch=1,
            grid=(bins // at_once,),
            in_specs=[
                pl.BlockSpec((groups, at_once, rows, gates), lambda b, counts: (0, b, 0, 0))
            ],
            out_specs=pl.BlockSpec((at_once, size // 4, size), lambda b, counts: (b, 0, 0)),
        ),
        out_shape=jax.ShapeDtypeStruct((bins, size // 4, size), jnp.float32),
        compiler_params=params(),
        cost_estimate=cost(2 * bins * size * size * gates, 2 * bins * size * gates),
        name="gram",
    )(counts, data)


def factor_kernel(groups, segment_ref, counts_ref, ridge_ref, grams_ref, out_ref, work_ref, inverse_ref):
    segments, bins, quarter, size = grams_ref.shape
    half = size // 2
    segment = segment_ref[0]
    lane = lax.broadcasted_iota(jnp.int32, (half, size), 1)
    row = lax.broadcasted_iota(jnp.int32, (size, size), 0)
    column = lax.broadcasted_iota(jnp.int32, (size, size), 1)
    inner_row = jnp.where(row < half, row, row - half)
    inner_column = jnp.where(column < half, column, column - half)
    lower = inner_row >= inner_column
    diagonal = inner_row == inner_column
    upper_side = jnp.logical_and(row < half, column >= half)
    lower_side = jnp.logical_and(row >= half, column < half)
    side = jnp.logical_or(upper_side, lower_side)
    for b in range(bins):
        total = grams_ref[0, b]
        for t in range(1, segments):
            total = jnp.where(t <= segment, total + grams_ref[t, b], total)
        packed = jnp.concatenate([total, pltpu.roll(total, half, 1)], axis=0)
        packed = jnp.where(lane < half, packed, pltpu.roll(packed, half, 1))
        packed = jnp.concatenate([packed, packed], axis=0)
        turned = packed.T
        symmetric = jnp.where(lower, packed, turned)
        skew = jnp.where(diagonal, 0.0, jnp.where(lower, -turned, packed))
        full = jnp.where(side, jnp.where(lower_side, -skew, skew), symmetric)
        used = ((segment + 1) * counts_ref[b] * TRAIN_BLK).astype(jnp.float32)
        covariance = full / used
        kept = jnp.logical_or(ridge_ref[b] == 1, row == column)
        work_ref[b] = jnp.where(kept, covariance, 0.0) + jnp.where(row == column, LOADING, 0.0)

    one_lane = lax.broadcasted_iota(jnp.int32, (1, size), 1)
    panel = min(PANEL if bins > 8 else 2 * PANEL, size)
    panel_lane = lax.broadcasted_iota(jnp.int32, (panel, size), 1)
    panel_row = lax.broadcasted_iota(jnp.int32, (panel, size), 0)
    for low in range(0, size, panel):
        high = low + panel

        def step(k, carry, low=low, high=high):
            j = low + 2 * k
            first_lane, second_lane = one_lane == j, one_lane == j + 1
            first_mask, second_mask = panel_lane == j, panel_lane == j + 1
            scales, units = [], []
            for b in range(bins):
                row = work_ref[b, pl.ds(j, 1), :]
                following = work_ref[b, pl.ds(j + 1, 1), :]
                pivot = jnp.sum(jnp.where(first_lane, row, 0.0), axis=1, keepdims=True)
                link = jnp.sum(jnp.where(second_lane, row, 0.0), axis=1, keepdims=True)
                corner = jnp.sum(jnp.where(second_lane, following, 0.0), axis=1, keepdims=True)
                root = lax.rsqrt(pivot)
                ratio = link * (root * root)
                second_root = lax.rsqrt(corner - ratio * link)
                unit = jnp.where(first_lane, 1.0, row)
                second = jnp.where(first_lane, 0.0, following) - ratio * unit
                second = jnp.where(second_lane, 1.0, second)
                scales.append((root, ratio, second_root))
                units.append((unit, second))
            for b in range(bins):
                root, ratio, second_root = scales[b]
                unit, second = units[b]
                inverse_ref[b, pl.ds(j, 1), :] = unit * root
                inverse_ref[b, pl.ds(j + 1, 1), :] = second * second_root
            for b in range(bins):
                root, ratio, second_root = scales[b]
                unit, second = units[b]
                matrix = work_ref[b, low:high, :]
                entries = jnp.sum(jnp.where(first_mask, matrix, 0.0), axis=1, keepdims=True)
                others = jnp.sum(jnp.where(second_mask, matrix, 0.0), axis=1, keepdims=True)
                others = (others - entries * ratio) * (second_root * second_root)
                entries = entries * (root * root)
                matrix = jnp.where(jnp.logical_or(first_mask, second_mask), 0.0, matrix)
                work_ref[b, low:high, :] = (
                    matrix - entries * jnp.where(second_lane, 0.0, unit) - others * second
                )
            return carry

        lax.fori_loop(0, panel // 2, step, 0)
        if high < size:
            inside = jnp.logical_and(panel_lane > panel_row + low, panel_lane < high)
            below_lane = lax.broadcasted_iota(jnp.int32, (size - high, size), 1)
            cleared = jnp.logical_and(below_lane >= low, below_lane < high)
            for b in range(bins):
                rows = inverse_ref[b, low:high, :]
                product = jnp.dot(
                    rows.T[high:],
                    jnp.where(inside, 0.0, rows),
                    preferred_element_type=jnp.float32,
                    precision=lax.Precision.HIGHEST,
                )
                work_ref[b, high:, :] = (
                    jnp.where(cleared, 0.0, work_ref[b, high:, :]) - product
                )
    for b in range(bins):
        inverse_ref[b] = jnp.where(column <= row, inverse_ref[b], 0.0)
    for b in range(bins):
        inverse = grouped_rows(inverse_ref[b].T, groups).T
        high = inverse.astype(jnp.bfloat16)
        out_ref[b, :size, :] = high
        out_ref[b, size:, :] = (inverse - high.astype(jnp.float32)).astype(jnp.bfloat16)


def inverse_factors(grams, segment, counts, ridge, groups):
    segments, bins, quarter, size = grams.shape
    smem = pl.BlockSpec(memory_space=pltpu.SMEM)
    return pl.pallas_call(
        functools.partial(factor_kernel, groups),
        in_specs=[smem, smem, smem, pl.BlockSpec(memory_space=pltpu.VMEM)],
        out_specs=pl.BlockSpec(memory_space=pltpu.VMEM),
        out_shape=jax.ShapeDtypeStruct((bins, 2 * size, size), jnp.bfloat16),
        scratch_shapes=[
            pltpu.VMEM((bins, size, size), jnp.float32),
            pltpu.VMEM((bins, size, size), jnp.float32),
        ],
        compiler_params=params(),
        cost_estimate=cost(2 * bins * size**3 * 20, 4 * segments * bins * quarter * size),
        name="inverse_factors",
    )(segment, counts, ridge, grams)


def whiten_kernel(inverse_ref, data_ref, *refs):
    out_ref = refs[-1]
    groups, bins, rows, gates = data_ref.shape
    size = groups * rows
    step = 1024 if gates % 1024 == 0 else gates
    for b in range(bins):
        for first in range(0, gates, step):
            data = data_ref[:, b, :, first : first + step].reshape(size, step)
            both = jnp.dot(inverse_ref[b], data, preferred_element_type=jnp.float32)
            out_ref[b, :, first : first + step] = (both[:size] + both[size:]).astype(out_ref.dtype)


def whiten(inverse, data, earlier, first, total):
    groups, bins, rows, gates = data.shape
    size = groups * rows
    at_once = next(k for k in (BINS_AT_ONCE, 2, 1) if bins % k == 0 and first % k == 0)
    in_specs = [
        pl.BlockSpec((at_once, 2 * size, size), lambda b: (b, 0, 0)),
        pl.BlockSpec((groups, at_once, rows, gates), lambda b: (0, b, 0, 0)),
    ]
    operands = [inverse, data]
    aliases = {}
    if earlier is not None:
        in_specs.append(pl.BlockSpec(memory_space=pl.ANY))
        operands.append(earlier)
        aliases = {2: 0}
    return pl.pallas_call(
        whiten_kernel,
        grid=(bins // at_once,),
        in_specs=in_specs,
        out_specs=pl.BlockSpec((at_once, size, gates), lambda b: (first // at_once + b, 0, 0)),
        out_shape=jax.ShapeDtypeStruct((total, size, gates), data.dtype),
        input_output_aliases=aliases,
        compiler_params=params(),
        cost_estimate=cost(4 * bins * size * size * gates, 4 * bins * size * gates),
        name="whiten",
    )(*operands)


def exchange(array):
    return lax.all_to_all(array, "dop", split_axis=0, concat_axis=0, tiled=True)


def per_device(echoes, chirp, ridge, counts):
    taps = chirp.shape[1]
    _, pulses, channels, gates = echoes.shape
    groups = lax.axis_size("dop")
    group = channels // groups
    pulse_count = pulses * groups
    bins = counts.shape[0]
    bin_plan = chunks(bins, BIN_PLAN)
    gate_plan = [
        (gates - taps * (start + size), taps * size)
        for start, size in chunks(gates // taps, GATE_PLAN)
    ]

    segments = lax.axis_size("rng")
    route = [(k, k + 1) for k in range(segments - 1)]
    halo = lax.ppermute(echoes[:, :, :, gates - taps :], "rng", route)
    table = filter_table(chirp)
    tables = doppler_tables(pulse_count, groups)

    received = []
    for start, size in gate_plan:
        received.append(exchange(compress(echoes, table, halo, start, size, groups)))

    if group % 8 == 0:
        spectra = None
        for (start, size), part in zip(gate_plan, received):
            spectra = doppler(part, tables, spectra, start, gates, bin_plan)
    else:
        pieces = [doppler_plain(part, tables, bin_plan) for part in received]
        spectra = [jnp.concatenate(piece[::-1], axis=3) for piece in zip(*pieces)]

    segment = lax.axis_index("rng").reshape(1)
    whitened = None
    data = exchange(spectra[0])
    for k, (first, count) in enumerate(bin_plan):
        if k + 1 < len(bin_plan):
            if whitened is None:
                following, data = lax.optimization_barrier((spectra[k + 1], data))
            else:
                following, data, whitened = lax.optimization_barrier(
                    (spectra[k + 1], data, whitened)
                )
            following = exchange(following)
        if group % 8:
            data = data.reshape(groups, count, 2, group, gates).transpose(1, 2, 0, 3, 4)
            data = data.reshape(1, count, 2 * channels, gates)
        these = counts[first : first + count]
        grams = lax.all_gather(gram(data, these), "rng")
        inverse = inverse_factors(
            grams, segment, these, ridge[first : first + count], data.shape[0]
        )
        whitened = whiten(inverse, data, whitened, first, bins)
        data = following
    return whitened


def solution(mesh):
    in_specs = (P(None, "dop", None, "rng"), P(), P("dop"), P("dop"))
    out_specs = P("dop", None, "rng")
    return jax.shard_map(
        per_device, mesh=mesh, in_specs=in_specs, out_specs=out_specs, check_vma=False
    )
```

```python
import functools
import math

import jax
import jax.numpy as jnp
import numpy as np
from jax import lax
from jax.experimental import pallas as pl
from jax.experimental.pallas import tpu as pltpu
from jax.sharding import PartitionSpec as P

TRAIN_BLK = 512
LOADING = 0.1
LANES = 128
BINS_AT_ONCE = 4
PANEL = 16
TILE = 128
WIDTH = 256
VMEM_LIMIT = 50 * 1024 * 1024

GATE_PLAN = (1, 6, 1)
BIN_PLAN = (12, 3, 1)


def params():
    return pltpu.CompilerParams(vmem_limit_bytes=VMEM_LIMIT)


def cost(flops, nbytes):
    return pl.CostEstimate(flops=int(flops), bytes_accessed=int(nbytes), transcendentals=0)


def chunks(total, plan):
    sizes = [max(1, total * part // sum(plan)) for part in plan]
    sizes[0] = total - sum(sizes[1:])
    starts = [sum(sizes[:k]) for k in range(len(sizes))]
    return list(zip(starts, sizes))


def table_kernel(taps, sequence_ref, table_ref):
    rows = taps + TILE
    length = sequence_ref.shape[1]
    tables = []
    for component in range(2):
        wide = jnp.broadcast_to(sequence_ref[component : component + 1, :], (rows, length))
        rolled = pltpu.roll(wide, 0, 1, stride=1, stride_axis=0)
        tables.append(rolled[:, :TILE])
    real, imag = tables
    table_ref[:rows, :TILE] = real.astype(table_ref.dtype)
    table_ref[:rows, TILE:] = imag.astype(table_ref.dtype)
    table_ref[rows:, :TILE] = (-imag).astype(table_ref.dtype)
    table_ref[rows:, TILE:] = real.astype(table_ref.dtype)


def filter_table(chirp):
    taps = chirp.shape[1]
    pad = taps + TILE - taps % TILE - TILE
    sequence = jnp.concatenate([jnp.zeros((2, pad), chirp.dtype), chirp], axis=1).astype(jnp.float32)
    return pl.pallas_call(
        functools.partial(table_kernel, taps),
        out_shape=jax.ShapeDtypeStruct((2 * (taps + TILE), 2 * TILE), chirp.dtype),
        compiler_params=params(),
        name="filter_table",
    )(sequence)


def compress_kernel(taps, has_halo, group, *refs):
    if has_halo:
        table_ref, halo_ref, before_ref, now_ref, out_ref, *slots = refs
    else:
        table_ref, before_ref, now_ref, out_ref, *slots = refs
    pulses, channels, gates = now_ref.shape[1:]
    rows = pulses * channels
    parts = []
    for component in range(2):
        before = before_ref[component]
        if has_halo:
            before = jnp.where(pl.program_id(1) == 0, halo_ref[component], before)
        parts.append(
            jnp.concatenate(
                [before.reshape(rows, taps), now_ref[component].reshape(rows, gates)], axis=1
            )
        )
    for tile in range(gates // TILE):
        first = tile * TILE
        wide_ref = slots[tile % len(slots)]
        window = jnp.concatenate([part[:, first : first + taps + TILE] for part in parts], axis=1)
        filtered = jnp.dot(window, table_ref[...], preferred_element_type=jnp.float32)
        per_part = TILE // LANES
        for lane_tile in range(2 * per_part):
            wide_ref[lane_tile, :rows] = filtered[:, lane_tile * LANES : (lane_tile + 1) * LANES]
        for channel in range(channels):
            for lane_tile in range(2 * per_part):
                component = lane_tile // per_part
                lanes = first + lane_tile % per_part * LANES
                piece = wide_ref[lane_tile, pl.ds(channel, pulses, stride=channels), :]
                out_ref[
                    channel // group,
                    channel % group,
                    component * pulses : (component + 1) * pulses,
                    lanes : lanes + LANES,
                ] = piece.astype(out_ref.dtype)


def compress(echoes, table, halo, start, size, groups):
    _, pulses, channels, gates = echoes.shape
    taps = table.shape[0] // 2 - TILE
    group = channels // groups
    at_once = max(16, group)
    step = taps
    offset = start // step
    has_halo = start == 0
    block = (2, pulses, at_once, step)
    in_specs = [pl.BlockSpec(table.shape, lambda c, g: (0, 0))]
    operands = [table]
    if has_halo:
        in_specs.append(pl.BlockSpec(block, lambda c, g: (0, 0, c, 0)))
        operands.append(halo)
    in_specs.append(pl.BlockSpec(block, lambda c, g: (0, 0, c, jnp.maximum(offset + g - 1, 0))))
    in_specs.append(pl.BlockSpec(block, lambda c, g: (0, 0, c, offset + g)))
    operands += [echoes, echoes]
    return pl.pallas_call(
        functools.partial(compress_kernel, taps, has_halo, group),
        grid=(channels // at_once, size // step),
        in_specs=in_specs,
        out_specs=pl.BlockSpec(
            (at_once // group, group, 2 * pulses, step), lambda c, g: (c, 0, 0, g)
        ),
        out_shape=jax.ShapeDtypeStruct((groups, group, 2 * pulses, size), echoes.dtype),
        scratch_shapes=[
            pltpu.VMEM((2 * TILE // LANES, (pulses + 1) * at_once, LANES), jnp.float32)
        ]
        * 2,
        compiler_params=params(),
        cost_estimate=cost(
            2 * pulses * channels * size * (taps + TILE) * 4, 12 * pulses * channels * size
        ),
        name="compress",
    )(*operands)


def doppler_tables(pulse_count, groups):
    index = np.arange(pulse_count, dtype=np.int64)
    angles = (index[:, None] * index[None, :] % pulse_count) * (2.0 * math.pi / pulse_count)
    cosine = np.cos(angles) / math.sqrt(pulse_count)
    sine = np.sin(angles) / math.sqrt(pulse_count)
    local = pulse_count // groups
    cosine = cosine.reshape(pulse_count, groups, 1, local)
    sine = sine.reshape(pulse_count, groups, 1, local)
    real_rows = np.concatenate([cosine, sine], axis=2).reshape(pulse_count, 2 * pulse_count)
    imag_rows = np.concatenate([-sine, cosine], axis=2).reshape(pulse_count, 2 * pulse_count)
    table = np.concatenate([real_rows, imag_rows], axis=0)
    high = table.astype(jnp.bfloat16)
    low = (table - high.astype(np.float64)).astype(jnp.bfloat16)
    return jnp.asarray(high), jnp.asarray(low)


def doppler_kernel(plan, carried, *refs):
    high_ref, low_ref, in_ref = refs[:3]
    outs = refs[3 + carried : 3 + carried + len(plan)]
    wide_ref = refs[-1]
    groups, group, depth, gates = in_ref.shape
    total = groups * depth
    bins = total // 2
    local = bins // groups
    for channel in range(group):
        data = in_ref[:, channel].reshape(total, gates)
        spectrum = jnp.dot(high_ref[...], data, preferred_element_type=jnp.float32)
        spectrum = spectrum + jnp.dot(low_ref[...], data, preferred_element_type=jnp.float32)
        for lane_tile in range(gates // LANES):
            wide_ref[lane_tile, pl.ds(channel, total, stride=group), :] = spectrum[
                :, lane_tile * LANES : (lane_tile + 1) * LANES
            ]
    for out_ref, (first, count) in zip(outs, plan):
        for place in range(groups):

            def move(k, carry, out_ref=out_ref, base=place * local + first, place=place):
                for lane_tile in range(gates // LANES):
                    real = wide_ref[lane_tile, pl.ds((base + k) * group, group), :]
                    imag = wide_ref[lane_tile, pl.ds((base + k + bins) * group, group), :]
                    out_ref[place, k, :, lane_tile * LANES : (lane_tile + 1) * LANES] = (
                        jnp.concatenate([real, imag], axis=0).astype(out_ref.dtype)
                    )
                return carry

            lax.fori_loop(0, count, move, 0, unroll=True)


def doppler(received, tables, earlier, start, gates, plan):
    groups, group, depth, size = received.shape
    total = groups * depth
    step = WIDTH
    offset = start // step
    table_spec = pl.BlockSpec((total, total), lambda g: (0, 0))
    in_specs = [
        table_spec,
        table_spec,
        pl.BlockSpec((groups, group, depth, step), lambda g: (0, 0, 0, g)),
    ]
    operands = [*tables, received]
    aliases = {}
    if earlier is not None:
        for k, array in enumerate(earlier):
            aliases[len(operands)] = k
            operands.append(array)
            in_specs.append(pl.BlockSpec(memory_space=pl.ANY))
    return pl.pallas_call(
        functools.partial(doppler_kernel, plan, 0 if earlier is None else len(earlier)),
        grid=(size // step,),
        in_specs=in_specs,
        out_specs=[
            pl.BlockSpec((groups, count, 2 * group, step), lambda g: (0, 0, 0, offset + g))
            for _, count in plan
        ],
        out_shape=[
            jax.ShapeDtypeStruct((groups, count, 2 * group, gates), received.dtype)
            for _, count in plan
        ],
        scratch_shapes=[pltpu.VMEM((step // LANES, group * (total + 1), LANES), jnp.float32)],
        input_output_aliases=aliases,
        compiler_params=params(),
        cost_estimate=cost(4 * total * total * group * size, 4 * total * group * size),
        name="doppler",
    )(*operands)


def doppler_plain(received, tables, plan):
    groups, group, depth, size = received.shape
    total = groups * depth
    data = jnp.moveaxis(received, 1, 2).reshape(total, group * size)
    spectrum = jnp.dot(tables[0], data, preferred_element_type=jnp.float32)
    spectrum = spectrum + jnp.dot(tables[1], data, preferred_element_type=jnp.float32)
    spectrum = spectrum.astype(received.dtype).reshape(2, groups, depth // 2, group, size)
    spectrum = spectrum.transpose(1, 2, 0, 3, 4).reshape(groups, depth // 2, 2 * group, size)
    return [spectrum[:, first : first + count] for first, count in plan]


def natural_rows(matrix, groups):
    half = matrix.shape[0] // groups // 2
    pieces = [matrix[2 * half * s : 2 * half * s + half] for s in range(groups)]
    pieces += [matrix[2 * half * s + half : 2 * half * (s + 1)] for s in range(groups)]
    return jnp.concatenate(pieces, axis=0)


def grouped_rows(matrix, groups):
    rows = matrix.shape[0]
    half = rows // groups // 2
    pieces = []
    for s in range(groups):
        pieces.append(matrix[half * s : half * (s + 1)])
        pieces.append(matrix[rows // 2 + half * s : rows // 2 + half * (s + 1)])
    return jnp.concatenate(pieces, axis=0)


def gram_kernel(counts_ref, data_ref, out_ref):
    groups, bins, rows, gates = data_ref.shape
    size = groups * rows
    half, quarter = size // 2, size // 4
    row = lax.broadcasted_iota(jnp.int32, (half, size), 0)
    lane = lax.broadcasted_iota(jnp.int32, (half, size), 1)
    gate = lax.broadcasted_iota(jnp.int32, (size, gates), 1)
    for b in range(bins):
        training = counts_ref[pl.program_id(0) * bins + b] * TRAIN_BLK
        data = data_ref[:, b].reshape(size, gates)
        data = jnp.where(gate < training, data, jnp.zeros_like(data))
        gram = lax.dot_general(
            data, data, (((1,), (1,)), ((), ())), preferred_element_type=jnp.float32
        )
        gram = natural_rows(natural_rows(gram, groups).T, groups)
        turned = pltpu.roll(gram[half:], half, 1)
        top = gram[:half] + jnp.where(lane < half, turned, -turned)
        packed = jnp.where(row >= lane, top, pltpu.roll(top, half, 1))
        out_ref[b] = jnp.where(
            lane[:quarter] < half, packed[:quarter], pltpu.roll(packed[quarter:], half, 1)
        )


def per_step(bins):
    return next(k for k in (BINS_AT_ONCE, 2, 1) if bins % k == 0)


def gram(data, counts):
    groups, bins, rows, gates = data.shape
    size = groups * rows
    at_once = per_step(bins)
    return pl.pallas_call(
        gram_kernel,
        grid_spec=pltpu.PrefetchScalarGridSpec(
            num_scalar_prefetch=1,
            grid=(bins // at_once,),
            in_specs=[
                pl.BlockSpec((groups, at_once, rows, gates), lambda b, counts: (0, b, 0, 0))
            ],
            out_specs=pl.BlockSpec((at_once, size // 4, size), lambda b, counts: (b, 0, 0)),
        ),
        out_shape=jax.ShapeDtypeStruct((bins, size // 4, size), jnp.float32),
        compiler_params=params(),
        cost_estimate=cost(2 * bins * size * size * gates, 2 * bins * size * gates),
        name="gram",
    )(counts, data)


def factor_kernel(groups, segment_ref, counts_ref, ridge_ref, grams_ref, out_ref, work_ref, inverse_ref):
    segments, bins, quarter, size = grams_ref.shape
    half = size // 2
    segment = segment_ref[0]
    lane = lax.broadcasted_iota(jnp.int32, (half, size), 1)
    row = lax.broadcasted_iota(jnp.int32, (size, size), 0)
    column = lax.broadcasted_iota(jnp.int32, (size, size), 1)
    inner_row = jnp.where(row < half, row, row - half)
    inner_column = jnp.where(column < half, column, column - half)
    lower = inner_row >= inner_column
    diagonal = inner_row == inner_column
    upper_side = jnp.logical_and(row < half, column >= half)
    lower_side = jnp.logical_and(row >= half, column < half)
    side = jnp.logical_or(upper_side, lower_side)
    for b in range(bins):
        total = grams_ref[0, b]
        for t in range(1, segments):
            total = jnp.where(t <= segment, total + grams_ref[t, b], total)
        packed = jnp.concatenate([total, pltpu.roll(total, half, 1)], axis=0)
        packed = jnp.where(lane < half, packed, pltpu.roll(packed, half, 1))
        packed = jnp.concatenate([packed, packed], axis=0)
        turned = packed.T
        symmetric = jnp.where(lower, packed, turned)
        skew = jnp.where(diagonal, 0.0, jnp.where(lower, -turned, packed))
        full = jnp.where(side, jnp.where(lower_side, -skew, skew), symmetric)
        used = ((segment + 1) * counts_ref[b] * TRAIN_BLK).astype(jnp.float32)
        covariance = full / used
        kept = jnp.logical_or(ridge_ref[b] == 1, row == column)
        work_ref[b] = jnp.where(kept, covariance, 0.0) + jnp.where(row == column, LOADING, 0.0)

    one_lane = lax.broadcasted_iota(jnp.int32, (1, size), 1)
    panel = min(PANEL if bins > 8 else 2 * PANEL, size)
    panel_lane = lax.broadcasted_iota(jnp.int32, (panel, size), 1)
    panel_row = lax.broadcasted_iota(jnp.int32, (panel, size), 0)
    for low in range(0, size, panel):
        high = low + panel

        def step(k, carry, low=low, high=high):
            j = low + 2 * k
            first_lane, second_lane = one_lane == j, one_lane == j + 1
            first_mask, second_mask = panel_lane == j, panel_lane == j + 1
            scales, units = [], []
            for b in range(bins):
                row = work_ref[b, pl.ds(j, 1), :]
                following = work_ref[b, pl.ds(j + 1, 1), :]
                pivot = jnp.sum(jnp.where(first_lane, row, 0.0), axis=1, keepdims=True)
                link = jnp.sum(jnp.where(second_lane, row, 0.0), axis=1, keepdims=True)
                corner = jnp.sum(jnp.where(second_lane, following, 0.0), axis=1, keepdims=True)
                root = lax.rsqrt(pivot)
                ratio = link * (root * root)
                second_root = lax.rsqrt(corner - ratio * link)
                unit = jnp.where(first_lane, 1.0, row)
                second = jnp.where(first_lane, 0.0, following) - ratio * unit
                second = jnp.where(second_lane, 1.0, second)
                scales.append((root, ratio, second_root))
                units.append((unit, second))
            for b in range(bins):
                root, ratio, second_root = scales[b]
                unit, second = units[b]
                inverse_ref[b, pl.ds(j, 1), :] = unit * root
                inverse_ref[b, pl.ds(j + 1, 1), :] = second * second_root
            for b in range(bins):
                root, ratio, second_root = scales[b]
                unit, second = units[b]
                matrix = work_ref[b, low:high, :]
                entries = jnp.sum(jnp.where(first_mask, matrix, 0.0), axis=1, keepdims=True)
                others = jnp.sum(jnp.where(second_mask, matrix, 0.0), axis=1, keepdims=True)
                others = (others - entries * ratio) * (second_root * second_root)
                entries = entries * (root * root)
                matrix = jnp.where(jnp.logical_or(first_mask, second_mask), 0.0, matrix)
                work_ref[b, low:high, :] = (
                    matrix - entries * jnp.where(second_lane, 0.0, unit) - others * second
                )
            return carry

        lax.fori_loop(0, panel // 2, step, 0)
        if high < size:
            inside = jnp.logical_and(panel_lane > panel_row + low, panel_lane < high)
            below_lane = lax.broadcasted_iota(jnp.int32, (size - high, size), 1)
            cleared = jnp.logical_and(below_lane >= low, below_lane < high)
            for b in range(bins):
                rows = inverse_ref[b, low:high, :]
                product = jnp.dot(
                    rows.T[high:],
                    jnp.where(inside, 0.0, rows),
                    preferred_element_type=jnp.float32,
                    precision=lax.Precision.HIGHEST,
                )
                work_ref[b, high:, :] = (
                    jnp.where(cleared, 0.0, work_ref[b, high:, :]) - product
                )
    for b in range(bins):
        inverse_ref[b] = jnp.where(column <= row, inverse_ref[b], 0.0)
    for b in range(bins):
        inverse = grouped_rows(inverse_ref[b].T, groups).T
        high = inverse.astype(jnp.bfloat16)
        out_ref[b, :size, :] = high
        out_ref[b, size:, :] = (inverse - high.astype(jnp.float32)).astype(jnp.bfloat16)


def inverse_factors(grams, segment, counts, ridge, groups):
    segments, bins, quarter, size = grams.shape
    smem = pl.BlockSpec(memory_space=pltpu.SMEM)
    return pl.pallas_call(
        functools.partial(factor_kernel, groups),
        in_specs=[smem, smem, smem, pl.BlockSpec(memory_space=pltpu.VMEM)],
        out_specs=pl.BlockSpec(memory_space=pltpu.VMEM),
        out_shape=jax.ShapeDtypeStruct((bins, 2 * size, size), jnp.bfloat16),
        scratch_shapes=[
            pltpu.VMEM((bins, size, size), jnp.float32),
            pltpu.VMEM((bins, size, size), jnp.float32),
        ],
        compiler_params=params(),
        cost_estimate=cost(2 * bins * size**3 * 20, 4 * segments * bins * quarter * size),
        name="inverse_factors",
    )(segment, counts, ridge, grams)


def whiten_kernel(inverse_ref, data_ref, *refs):
    out_ref = refs[-1]
    groups, bins, rows, gates = data_ref.shape
    size = groups * rows
    step = 1024 if gates % 1024 == 0 else gates
    for b in range(bins):
        for first in range(0, gates, step):
            data = data_ref[:, b, :, first : first + step].reshape(size, step)
            both = jnp.dot(inverse_ref[b], data, preferred_element_type=jnp.float32)
            out_ref[b, :, first : first + step] = (both[:size] + both[size:]).astype(out_ref.dtype)


def whiten(inverse, data, earlier, first, total):
    groups, bins, rows, gates = data.shape
    size = groups * rows
    at_once = next(k for k in (BINS_AT_ONCE, 2, 1) if bins % k == 0 and first % k == 0)
    in_specs = [
        pl.BlockSpec((at_once, 2 * size, size), lambda b: (b, 0, 0)),
        pl.BlockSpec((groups, at_once, rows, gates), lambda b: (0, b, 0, 0)),
    ]
    operands = [inverse, data]
    aliases = {}
    if earlier is not None:
        in_specs.append(pl.BlockSpec(memory_space=pl.ANY))
        operands.append(earlier)
        aliases = {2: 0}
    return pl.pallas_call(
        whiten_kernel,
        grid=(bins // at_once,),
        in_specs=in_specs,
        out_specs=pl.BlockSpec((at_once, size, gates), lambda b: (first // at_once + b, 0, 0)),
        out_shape=jax.ShapeDtypeStruct((total, size, gates), data.dtype),
        input_output_aliases=aliases,
        compiler_params=params(),
        cost_estimate=cost(4 * bins * size * size * gates, 4 * bins * size * gates),
        name="whiten",
    )(*operands)


def exchange(array):
    return lax.all_to_all(array, "dop", split_axis=0, concat_axis=0, tiled=True)


def per_device(echoes, chirp, ridge, counts):
    taps = chirp.shape[1]
    _, pulses, channels, gates = echoes.shape
    groups = lax.axis_size("dop")
    group = channels // groups
    pulse_count = pulses * groups
    bins = counts.shape[0]
    bin_plan = chunks(bins, BIN_PLAN)
    gate_plan = [
        (gates - taps * (start + size), taps * size)
        for start, size in chunks(gates // taps, GATE_PLAN)
    ]

    segments = lax.axis_size("rng")
    route = [(k, k + 1) for k in range(segments - 1)]
    halo = lax.ppermute(echoes[:, :, :, gates - taps :], "rng", route)
    table = filter_table(chirp)
    tables = doppler_tables(pulse_count, groups)

    received = []
    for start, size in gate_plan:
        received.append(exchange(compress(echoes, table, halo, start, size, groups)))

    if group % 8 == 0:
        spectra = None
        for (start, size), part in zip(gate_plan, received):
            spectra = doppler(part, tables, spectra, start, gates, bin_plan)
    else:
        pieces = [doppler_plain(part, tables, bin_plan) for part in received]
        spectra = [jnp.concatenate(piece[::-1], axis=3) for piece in zip(*pieces)]

    segment = lax.axis_index("rng").reshape(1)
    whitened = None
    data = exchange(spectra[0])
    for k, (first, count) in enumerate(bin_plan):
        if k + 1 < len(bin_plan):
            if whitened is None:
                following, data = lax.optimization_barrier((spectra[k + 1], data))
            else:
                following, data, whitened = lax.optimization_barrier(
                    (spectra[k + 1], data, whitened)
                )
            following = exchange(following)
        if group % 8:
            data = data.reshape(groups, count, 2, group, gates).transpose(1, 2, 0, 3, 4)
            data = data.reshape(1, count, 2 * channels, gates)
        these = counts[first : first + count]
        grams = lax.all_gather(gram(data, these), "rng")
        inverse = inverse_factors(
            grams, segment, these, ridge[first : first + count], data.shape[0]
        )
        whitened = whiten(inverse, data, whitened, first, bins)
        data = following
    return whitened


def solution(mesh):
    in_specs = (P(None, "dop", None, "rng"), P(), P("dop"), P("dop"))
    out_specs = P("dop", None, "rng")
    return jax.shard_map(
        per_device, mesh=mesh, in_specs=in_specs, out_specs=out_specs, check_vma=False
    )
```

```python
import functools
import math

import jax
import jax.numpy as jnp
import numpy as np
from jax import lax
from jax.experimental import pallas as pl
from jax.experimental.pallas import tpu as pltpu
from jax.sharding import PartitionSpec as P

TRAIN_BLK = 512
LOADING = 0.1
LANES = 128
BINS_AT_ONCE = 4
PANEL = 16
TILE = 128
WIDTH = 256
VMEM_LIMIT = 50 * 1024 * 1024

GATE_PLAN = (1, 6, 1)
BIN_PLAN = (12, 3, 1)


def params():
    return pltpu.CompilerParams(vmem_limit_bytes=VMEM_LIMIT)


def cost(flops, nbytes):
    return pl.CostEstimate(flops=int(flops), bytes_accessed=int(nbytes), transcendentals=0)


def chunks(total, plan):
    sizes = [max(1, total * part // sum(plan)) for part in plan]
    sizes[0] = total - sum(sizes[1:])
    starts = [sum(sizes[:k]) for k in range(len(sizes))]
    return list(zip(starts, sizes))


def table_kernel(taps, sequence_ref, table_ref):
    rows = taps + TILE
    length = sequence_ref.shape[1]
    tables = []
    for component in range(2):
        wide = jnp.broadcast_to(sequence_ref[component : component + 1, :], (rows, length))
        rolled = pltpu.roll(wide, 0, 1, stride=1, stride_axis=0)
        tables.append(rolled[:, :TILE])
    real, imag = tables
    table_ref[:rows, :TILE] = real.astype(table_ref.dtype)
    table_ref[:rows, TILE:] = imag.astype(table_ref.dtype)
    table_ref[rows:, :TILE] = (-imag).astype(table_ref.dtype)
    table_ref[rows:, TILE:] = real.astype(table_ref.dtype)


def filter_table(chirp):
    taps = chirp.shape[1]
    pad = taps + TILE - taps % TILE - TILE
    sequence = jnp.concatenate([jnp.zeros((2, pad), chirp.dtype), chirp], axis=1).astype(jnp.float32)
    return pl.pallas_call(
        functools.partial(table_kernel, taps),
        out_shape=jax.ShapeDtypeStruct((2 * (taps + TILE), 2 * TILE), chirp.dtype),
        compiler_params=params(),
        name="filter_table",
    )(sequence)


def compress_kernel(taps, has_halo, group, *refs):
    if has_halo:
        table_ref, halo_ref, before_ref, now_ref, out_ref, *slots = refs
    else:
        table_ref, before_ref, now_ref, out_ref, *slots = refs
    pulses, channels, gates = now_ref.shape[1:]
    rows = pulses * channels
    parts = []
    for component in range(2):
        before = before_ref[component]
        if has_halo:
            before = jnp.where(pl.program_id(1) == 0, halo_ref[component], before)
        parts.append(
            jnp.concatenate(
                [before.reshape(rows, taps), now_ref[component].reshape(rows, gates)], axis=1
            )
        )
    for tile in range(gates // TILE):
        first = tile * TILE
        wide_ref = slots[tile % len(slots)]
        window = jnp.concatenate([part[:, first : first + taps + TILE] for part in parts], axis=1)
        filtered = jnp.dot(window, table_ref[...], preferred_element_type=jnp.float32)
        per_part = TILE // LANES
        for lane_tile in range(2 * per_part):
            wide_ref[lane_tile, :rows] = filtered[:, lane_tile * LANES : (lane_tile + 1) * LANES]
        for channel in range(channels):
            for lane_tile in range(2 * per_part):
                component = lane_tile // per_part
                lanes = first + lane_tile % per_part * LANES
                piece = wide_ref[lane_tile, pl.ds(channel, pulses, stride=channels), :]
                out_ref[
                    channel // group,
                    channel % group,
                    component * pulses : (component + 1) * pulses,
                    lanes : lanes + LANES,
                ] = piece.astype(out_ref.dtype)


def compress(echoes, table, halo, start, size, groups):
    _, pulses, channels, gates = echoes.shape
    taps = table.shape[0] // 2 - TILE
    group = channels // groups
    at_once = max(16, group)
    step = taps
    offset = start // step
    has_halo = start == 0
    block = (2, pulses, at_once, step)
    in_specs = [pl.BlockSpec(table.shape, lambda c, g: (0, 0))]
    operands = [table]
    if has_halo:
        in_specs.append(pl.BlockSpec(block, lambda c, g: (0, 0, c, 0)))
        operands.append(halo)
    in_specs.append(pl.BlockSpec(block, lambda c, g: (0, 0, c, jnp.maximum(offset + g - 1, 0))))
    in_specs.append(pl.BlockSpec(block, lambda c, g: (0, 0, c, offset + g)))
    operands += [echoes, echoes]
    return pl.pallas_call(
        functools.partial(compress_kernel, taps, has_halo, group),
        grid=(channels // at_once, size // step),
        in_specs=in_specs,
        out_specs=pl.BlockSpec(
            (at_once // group, group, 2 * pulses, step), lambda c, g: (c, 0, 0, g)
        ),
        out_shape=jax.ShapeDtypeStruct((groups, group, 2 * pulses, size), echoes.dtype),
        scratch_shapes=[
            pltpu.VMEM((2 * TILE // LANES, (pulses + 1) * at_once, LANES), jnp.float32)
        ]
        * 2,
        compiler_params=params(),
        cost_estimate=cost(
            2 * pulses * channels * size * (taps + TILE) * 4, 12 * pulses * channels * size
        ),
        name="compress",
    )(*operands)


def doppler_tables(pulse_count, groups):
    index = np.arange(pulse_count, dtype=np.int64)
    angles = (index[:, None] * index[None, :] % pulse_count) * (2.0 * math.pi / pulse_count)
    cosine = np.cos(angles) / math.sqrt(pulse_count)
    sine = np.sin(angles) / math.sqrt(pulse_count)
    local = pulse_count // groups
    cosine = cosine.reshape(pulse_count, groups, 1, local)
    sine = sine.reshape(pulse_count, groups, 1, local)
    real_rows = np.concatenate([cosine, sine], axis=2).reshape(pulse_count, 2 * pulse_count)
    imag_rows = np.concatenate([-sine, cosine], axis=2).reshape(pulse_count, 2 * pulse_count)
    table = np.concatenate([real_rows, imag_rows], axis=0)
    high = table.astype(jnp.bfloat16)
    low = (table - high.astype(np.float64)).astype(jnp.bfloat16)
    return jnp.asarray(high), jnp.asarray(low)


def doppler_kernel(plan, carried, *refs):
    high_ref, low_ref, in_ref = refs[:3]
    outs = refs[3 + carried : 3 + carried + len(plan)]
    wide_ref = refs[-1]
    groups, group, depth, gates = in_ref.shape
    total = groups * depth
    bins = total // 2
    local = bins // groups
    for channel in range(group):
        data = in_ref[:, channel].reshape(total, gates)
        spectrum = jnp.dot(high_ref[...], data, preferred_element_type=jnp.float32)
        spectrum = spectrum + jnp.dot(low_ref[...], data, preferred_element_type=jnp.float32)
        for lane_tile in range(gates // LANES):
            wide_ref[lane_tile, pl.ds(channel, total, stride=group), :] = spectrum[
                :, lane_tile * LANES : (lane_tile + 1) * LANES
            ]
    for out_ref, (first, count) in zip(outs, plan):
        for place in range(groups):

            def move(k, carry, out_ref=out_ref, base=place * local + first, place=place):
                for lane_tile in range(gates // LANES):
                    real = wide_ref[lane_tile, pl.ds((base + k) * group, group), :]
                    imag = wide_ref[lane_tile, pl.ds((base + k + bins) * group, group), :]
                    out_ref[place, k, :, lane_tile * LANES : (lane_tile + 1) * LANES] = (
                        jnp.concatenate([real, imag], axis=0).astype(out_ref.dtype)
                    )
                return carry

            lax.fori_loop(0, count, move, 0, unroll=True)


def doppler(received, tables, earlier, start, gates, plan):
    groups, group, depth, size = received.shape
    total = groups * depth
    step = WIDTH
    offset = start // step
    table_spec = pl.BlockSpec((total, total), lambda g: (0, 0))
    in_specs = [
        table_spec,
        table_spec,
        pl.BlockSpec((groups, group, depth, step), lambda g: (0, 0, 0, g)),
    ]
    operands = [*tables, received]
    aliases = {}
    if earlier is not None:
        for k, array in enumerate(earlier):
            aliases[len(operands)] = k
            operands.append(array)
            in_specs.append(pl.BlockSpec(memory_space=pl.ANY))
    return pl.pallas_call(
        functools.partial(doppler_kernel, plan, 0 if earlier is None else len(earlier)),
        grid=(size // step,),
        in_specs=in_specs,
        out_specs=[
            pl.BlockSpec((groups, count, 2 * group, step), lambda g: (0, 0, 0, offset + g))
            for _, count in plan
        ],
        out_shape=[
            jax.ShapeDtypeStruct((groups, count, 2 * group, gates), received.dtype)
            for _, count in plan
        ],
        scratch_shapes=[pltpu.VMEM((step // LANES, group * (total + 1), LANES), jnp.float32)],
        input_output_aliases=aliases,
        compiler_params=params(),
        cost_estimate=cost(4 * total * total * group * size, 4 * total * group * size),
        name="doppler",
    )(*operands)


def doppler_plain(received, tables, plan):
    groups, group, depth, size = received.shape
    total = groups * depth
    data = jnp.moveaxis(received, 1, 2).reshape(total, group * size)
    spectrum = jnp.dot(tables[0], data, preferred_element_type=jnp.float32)
    spectrum = spectrum + jnp.dot(tables[1], data, preferred_element_type=jnp.float32)
    spectrum = spectrum.astype(received.dtype).reshape(2, groups, depth // 2, group, size)
    spectrum = spectrum.transpose(1, 2, 0, 3, 4).reshape(groups, depth // 2, 2 * group, size)
    return [spectrum[:, first : first + count] for first, count in plan]


def natural_rows(matrix, groups):
    half = matrix.shape[0] // groups // 2
    pieces = [matrix[2 * half * s : 2 * half * s + half] for s in range(groups)]
    pieces += [matrix[2 * half * s + half : 2 * half * (s + 1)] for s in range(groups)]
    return jnp.concatenate(pieces, axis=0)


def grouped_rows(matrix, groups):
    rows = matrix.shape[0]
    half = rows // groups // 2
    pieces = []
    for s in range(groups):
        pieces.append(matrix[half * s : half * (s + 1)])
        pieces.append(matrix[rows // 2 + half * s : rows // 2 + half * (s + 1)])
    return jnp.concatenate(pieces, axis=0)


def gram_kernel(counts_ref, data_ref, out_ref):
    groups, bins, rows, gates = data_ref.shape
    size = groups * rows
    half, quarter = size // 2, size // 4
    row = lax.broadcasted_iota(jnp.int32, (half, size), 0)
    lane = lax.broadcasted_iota(jnp.int32, (half, size), 1)
    gate = lax.broadcasted_iota(jnp.int32, (size, gates), 1)
    for b in range(bins):
        training = counts_ref[pl.program_id(0) * bins + b] * TRAIN_BLK
        data = data_ref[:, b].reshape(size, gates)
        data = jnp.where(gate < training, data, jnp.zeros_like(data))
        gram = lax.dot_general(
            data, data, (((1,), (1,)), ((), ())), preferred_element_type=jnp.float32
        )
        gram = natural_rows(natural_rows(gram, groups).T, groups)
        turned = pltpu.roll(gram[half:], half, 1)
        top = gram[:half] + jnp.where(lane < half, turned, -turned)
        packed = jnp.where(row >= lane, top, pltpu.roll(top, half, 1))
        out_ref[b] = jnp.where(
            lane[:quarter] < half, packed[:quarter], pltpu.roll(packed[quarter:], half, 1)
        )


def per_step(bins):
    return next(k for k in (BINS_AT_ONCE, 2, 1) if bins % k == 0)


def gram(data, counts):
    groups, bins, rows, gates = data.shape
    size = groups * rows
    at_once = per_step(bins)
    return pl.pallas_call(
        gram_kernel,
        grid_spec=pltpu.PrefetchScalarGridSpec(
            num_scalar_prefetch=1,
            grid=(bins // at_once,),
            in_specs=[
                pl.BlockSpec((groups, at_once, rows, gates), lambda b, counts: (0, b, 0, 0))
            ],
            out_specs=pl.BlockSpec((at_once, size // 4, size), lambda b, counts: (b, 0, 0)),
        ),
        out_shape=jax.ShapeDtypeStruct((bins, size // 4, size), jnp.float32),
        compiler_params=params(),
        cost_estimate=cost(2 * bins * size * size * gates, 2 * bins * size * gates),
        name="gram",
    )(counts, data)


def factor_kernel(groups, segment_ref, counts_ref, ridge_ref, grams_ref, out_ref, work_ref, inverse_ref):
    segments, bins, quarter, size = grams_ref.shape
    half = size // 2
    segment = segment_ref[0]
    lane = lax.broadcasted_iota(jnp.int32, (half, size), 1)
    row = lax.broadcasted_iota(jnp.int32, (size, size), 0)
    column = lax.broadcasted_iota(jnp.int32, (size, size), 1)
    inner_row = jnp.where(row < half, row, row - half)
    inner_column = jnp.where(column < half, column, column - half)
    lower = inner_row >= inner_column
    diagonal = inner_row == inner_column
    upper_side = jnp.logical_and(row < half, column >= half)
    lower_side = jnp.logical_and(row >= half, column < half)
    side = jnp.logical_or(upper_side, lower_side)
    for b in range(bins):
        total = grams_ref[0, b]
        for t in range(1, segments):
            total = jnp.where(t <= segment, total + grams_ref[t, b], total)
        packed = jnp.concatenate([total, pltpu.roll(total, half, 1)], axis=0)
        packed = jnp.where(lane < half, packed, pltpu.roll(packed, half, 1))
        packed = jnp.concatenate([packed, packed], axis=0)
        turned = packed.T
        symmetric = jnp.where(lower, packed, turned)
        skew = jnp.where(diagonal, 0.0, jnp.where(lower, -turned, packed))
        full = jnp.where(side, jnp.where(lower_side, -skew, skew), symmetric)
        used = ((segment + 1) * counts_ref[b] * TRAIN_BLK).astype(jnp.float32)
        covariance = full / used
        kept = jnp.logical_or(ridge_ref[b] == 1, row == column)
        work_ref[b] = jnp.where(kept, covariance, 0.0) + jnp.where(row == column, LOADING, 0.0)

    one_lane = lax.broadcasted_iota(jnp.int32, (1, size), 1)
    panel = min(PANEL if bins > 8 else 2 * PANEL, size)
    panel_lane = lax.broadcasted_iota(jnp.int32, (panel, size), 1)
    panel_row = lax.broadcasted_iota(jnp.int32, (panel, size), 0)
    for low in range(0, size, panel):
        high = low + panel

        def step(k, carry, low=low, high=high):
            j = low + 2 * k
            first_lane, second_lane = one_lane == j, one_lane == j + 1
            first_mask, second_mask = panel_lane == j, panel_lane == j + 1
            scales, units = [], []
            for b in range(bins):
                row = work_ref[b, pl.ds(j, 1), :]
                following = work_ref[b, pl.ds(j + 1, 1), :]
                pivot = jnp.sum(jnp.where(first_lane, row, 0.0), axis=1, keepdims=True)
                link = jnp.sum(jnp.where(second_lane, row, 0.0), axis=1, keepdims=True)
                corner = jnp.sum(jnp.where(second_lane, following, 0.0), axis=1, keepdims=True)
                root = lax.rsqrt(pivot)
                ratio = link * (root * root)
                second_root = lax.rsqrt(corner - ratio * link)
                unit = jnp.where(first_lane, 1.0, row)
                second = jnp.where(first_lane, 0.0, following) - ratio * unit
                second = jnp.where(second_lane, 1.0, second)
                scales.append((root, ratio, second_root))
                units.append((unit, second))
            for b in range(bins):
                root, ratio, second_root = scales[b]
                unit, second = units[b]
                inverse_ref[b, pl.ds(j, 1), :] = unit * root
                inverse_ref[b, pl.ds(j + 1, 1), :] = second * second_root
            for b in range(bins):
                root, ratio, second_root = scales[b]
                unit, second = units[b]
                matrix = work_ref[b, low:high, :]
                entries = jnp.sum(jnp.where(first_mask, matrix, 0.0), axis=1, keepdims=True)
                others = jnp.sum(jnp.where(second_mask, matrix, 0.0), axis=1, keepdims=True)
                others = (others - entries * ratio) * (second_root * second_root)
                entries = entries * (root * root)
                matrix = jnp.where(jnp.logical_or(first_mask, second_mask), 0.0, matrix)
                work_ref[b, low:high, :] = (
                    matrix - entries * jnp.where(second_lane, 0.0, unit) - others * second
                )
            return carry

        lax.fori_loop(0, panel // 2, step, 0)
        if high < size:
            inside = jnp.logical_and(panel_lane > panel_row + low, panel_lane < high)
            below_lane = lax.broadcasted_iota(jnp.int32, (size - high, size), 1)
            cleared = jnp.logical_and(below_lane >= low, below_lane < high)
            for b in range(bins):
                rows = inverse_ref[b, low:high, :]
                product = jnp.dot(
                    rows.T[high:],
                    jnp.where(inside, 0.0, rows),
                    preferred_element_type=jnp.float32,
                    precision=lax.Precision.HIGHEST,
                )
                work_ref[b, high:, :] = (
                    jnp.where(cleared, 0.0, work_ref[b, high:, :]) - product
                )
    for b in range(bins):
        inverse_ref[b] = jnp.where(column <= row, inverse_ref[b], 0.0)
    for b in range(bins):
        inverse = grouped_rows(inverse_ref[b].T, groups).T
        high = inverse.astype(jnp.bfloat16)
        out_ref[b, :size, :] = high
        out_ref[b, size:, :] = (inverse - high.astype(jnp.float32)).astype(jnp.bfloat16)


def whiten_kernel(segment_ref, counts_ref, ridge_ref, grams_ref, data_ref, *refs):
    out_ref, work_ref, inverse_ref, solved_ref = refs[-4:]
    groups, bins, rows, gates = data_ref.shape
    size = groups * rows

    @pl.when(pl.program_id(0) == 0)
    def _():
        factor_kernel(
            groups, segment_ref, counts_ref, ridge_ref, grams_ref, solved_ref, work_ref, inverse_ref
        )

    step = 1024 if gates % 1024 == 0 else gates
    for b in range(bins):
        inverse = solved_ref[pl.program_id(0) * bins + b]
        for first in range(0, gates, step):
            data = data_ref[:, b, :, first : first + step].reshape(size, step)
            both = jnp.dot(inverse, data, preferred_element_type=jnp.float32)
            out_ref[b, :, first : first + step] = (both[:size] + both[size:]).astype(out_ref.dtype)


def whiten(grams, segment, counts, ridge, data, earlier, first, total):
    groups, bins, rows, gates = data.shape
    size = groups * rows
    at_once = next(k for k in (BINS_AT_ONCE, 2, 1) if bins % k == 0 and first % k == 0)
    smem = pl.BlockSpec(memory_space=pltpu.SMEM)
    in_specs = [
        smem,
        smem,
        smem,
        pl.BlockSpec(grams.shape, lambda b: (0, 0, 0, 0)),
        pl.BlockSpec((groups, at_once, rows, gates), lambda b: (0, b, 0, 0)),
    ]
    operands = [segment, counts, ridge, grams, data]
    aliases = {}
    if earlier is not None:
        in_specs.append(pl.BlockSpec(memory_space=pl.ANY))
        operands.append(earlier)
        aliases = {5: 0}
    return pl.pallas_call(
        whiten_kernel,
        grid=(bins // at_once,),
        in_specs=in_specs,
        out_specs=pl.BlockSpec((at_once, size, gates), lambda b: (first // at_once + b, 0, 0)),
        out_shape=jax.ShapeDtypeStruct((total, size, gates), data.dtype),
        scratch_shapes=[
            pltpu.VMEM((bins, size, size), jnp.float32),
            pltpu.VMEM((bins, size, size), jnp.float32),
            pltpu.VMEM((bins, 2 * size, size), jnp.bfloat16),
        ],
        input_output_aliases=aliases,
        compiler_params=params(),
        cost_estimate=cost(
            4 * bins * size * size * gates + 40 * bins * size**3, 4 * bins * size * gates
        ),
        name="whiten",
    )(*operands)


def exchange(array):
    return lax.all_to_all(array, "dop", split_axis=0, concat_axis=0, tiled=True)


def per_device(echoes, chirp, ridge, counts):
    taps = chirp.shape[1]
    _, pulses, channels, gates = echoes.shape
    groups = lax.axis_size("dop")
    group = channels // groups
    pulse_count = pulses * groups
    bins = counts.shape[0]
    bin_plan = chunks(bins, BIN_PLAN)
    gate_plan = [
        (gates - taps * (start + size), taps * size)
        for start, size in chunks(gates // taps, GATE_PLAN)
    ]

    segments = lax.axis_size("rng")
    route = [(k, k + 1) for k in range(segments - 1)]
    halo = lax.ppermute(echoes[:, :, :, gates - taps :], "rng", route)
    table = filter_table(chirp)
    tables = doppler_tables(pulse_count, groups)

    received = []
    for start, size in gate_plan:
        received.append(exchange(compress(echoes, table, halo, start, size, groups)))

    if group % 8 == 0:
        spectra = None
        for (start, size), part in zip(gate_plan, received):
            spectra = doppler(part, tables, spectra, start, gates, bin_plan)
    else:
        pieces = [doppler_plain(part, tables, bin_plan) for part in received]
        spectra = [jnp.concatenate(piece[::-1], axis=3) for piece in zip(*pieces)]

    segment = lax.axis_index("rng").reshape(1)
    whitened = None
    data = exchange(spectra[0])
    for k, (first, count) in enumerate(bin_plan):
        if k + 1 < len(bin_plan):
            if whitened is None:
                following, data = lax.optimization_barrier((spectra[k + 1], data))
            else:
                following, data, whitened = lax.optimization_barrier(
                    (spectra[k + 1], data, whitened)
                )
            following = exchange(following)
        if group % 8:
            data = data.reshape(groups, count, 2, group, gates).transpose(1, 2, 0, 3, 4)
            data = data.reshape(1, count, 2 * channels, gates)
        these = counts[first : first + count]
        grams = lax.all_gather(gram(data, these), "rng")
        whitened = whiten(
            grams, segment, these, ridge[first : first + count], data, whitened, first, bins
        )
        data = following
    return whitened


def solution(mesh):
    in_specs = (P(None, "dop", None, "rng"), P(), P("dop"), P("dop"))
    out_specs = P("dop", None, "rng")
    return jax.shard_map(
        per_device, mesh=mesh, in_specs=in_specs, out_specs=out_specs, check_vma=False
    )
```
